32 devices in a mesh: rep: 4 (over x, core), fsdp: 8 (over z, y).
Axes of the slice: x: 2, y: 2, z: 4, core: 2. Of those that a mesh axis runs over, the one named last changes fastest.
Arguments:
- tokens: bfloat16 [512, 4096], P(('rep', 'fsdp')), may hold values from -6 to 6
- readout: bfloat16 [512, 14336], P('rep', 'fsdp'), may hold values from -0.046875 to 0.046875
- resp_mask: int32 [512], P('rep'), may hold values 0 or 1
- order: int32 [4, 8], P('rep'), may hold values from 0 to 7, each once within a row
- w_gate: bfloat16 [4, 14336, 4096], P('rep', 'fsdp'), may hold values from -0.09375 to 0.09375
- w_up: bfloat16 [4, 14336, 4096], P('rep', 'fsdp'), may hold values from -0.09375 to 0.09375
- outer_gate: bfloat16 [14336, 4096], P('fsdp', 'rep'), may hold values from -0.09375 to 0.09375
- outer_up: bfloat16 [14336, 4096], P('fsdp', 'rep'), may hold values from -0.09375 to 0.09375
- moment: float32 [14336, 4096], P('fsdp', 'rep'), may hold values from -0.09375 to 0.09375
Outputs:
- loss: float32 [4], P('rep')
- grad_gate: bfloat16 [4, 14336, 4096], P('rep', 'fsdp')
- grad_up: bfloat16 [4, 14336, 4096], P('rep', 'fsdp')
- new_outer: bfloat16 [14336, 4096], P('fsdp', 'rep')
- new_moment: float32 [14336, 4096], P('fsdp', 'rep')
The draws below stay inside these ranges and needn't reach their ends.
Inputs may be any that keep to these rules, and one draw needn't show every extreme that they name: Each row of order holds every sequence number of its group once.
All inputs are finite; a program needn't handle non-finite values. Where the reference program divides by a largest or mean magnitude, that divisor is 1e-20 or more. No bound on the sum of `resp_mask` on one device may be relied on, other than what follows from the above.
Results may differ from the reference program's by a relative error of at most 0.022.
Values may be sent and summed in bfloat16 or wider, within the bound.
No kernel may reach another device: no remote copies, remote signals or barrier semaphores. Data moves between devices by JAX's collectives and lax.ppermute only.
A program may use at most 256 MiB of HBM per device.

```python
import jax
import jax.numpy as jnp

D = 4096
FF = 14336
BLOCK = 128
LEN = 16
REPS = 4
GROUP_TOK = 128
SEQS = 8
PAIRS = 4
TOKENS = 512


def place_ends(values, rng, low, top_value):
    spot = [jax.random.randint(jax.random.fold_in(rng, axis), (), 0, length) for axis, length in enumerate(values.shape)]
    main_axis = values.shape.index(max(values.shape))
    neighbour = spot[:main_axis] + [(spot[main_axis] + 1) % values.shape[main_axis]] + spot[main_axis + 1:]
    return values.at[tuple(spot)].set(low).at[tuple(neighbour)].set(top_value)


def block_levels(key, dims, split, low, largest):
    level = 1.0
    for dim, blocks in split:
        heights = jax.random.uniform(jax.random.fold_in(jax.random.fold_in(key, 6), dim), (blocks,), jnp.float32, low / len(split), largest / len(split))
        level = level * jnp.repeat(jnp.exp(heights), dims[dim] // blocks).reshape((-1,) + (1,) * (len(dims) - 1 - dim))
    return level


def normal_values(rng, extent, deviation, bound, cuts=(), held_as=jnp.bfloat16):
    result = deviation * jax.random.normal(rng, extent, jnp.float32)
    if cuts:
        result = result * block_levels(rng, extent, cuts, -0.22, 0.18)
    return jnp.clip(result, -bound, bound).astype(held_as)


def setup_inputs(seed: int = 0) -> dict:
    keys = jax.random.split(jax.random.key(seed), 10)
    tokens = normal_values(keys[0], (TOKENS, D), 1.0, 6.0, ((0, 32),))
    readout = normal_values(keys[1], (TOKENS, FF), FF ** -0.5, 0.046875, ((0, 4), (1, 8)))
    resp_mask = place_ends((jax.random.randint(keys[2], (TOKENS,), 0, 4) < 3).astype(jnp.int32), jax.random.fold_in(keys[2], 1), 0, 1)
    order = jax.vmap(lambda own: jax.random.permutation(own, SEQS))(jax.random.split(keys[3], REPS)).reshape((REPS, SEQS)).astype(jnp.int32)
    w_gate = normal_values(keys[4], (REPS, FF, D), D ** -0.5, 0.09375, ((0, 4), (1, 8)))
    w_up = normal_values(keys[5], (REPS, FF, D), D ** -0.5, 0.09375, ((0, 4), (1, 8)))
    outer_gate = normal_values(keys[6], (FF, D), D ** -0.5, 0.09375, ((0, 8), (1, 4)))
    outer_up = normal_values(keys[7], (FF, D), D ** -0.5, 0.09375, ((0, 8), (1, 4)))
    moment = normal_values(keys[8], (FF, D), D ** -0.5, 0.09375, ((0, 8), (1, 4)), jnp.float32)
    return dict(tokens=tokens, readout=readout, resp_mask=resp_mask, order=order, w_gate=w_gate, w_up=w_up, outer_gate=outer_gate, outer_up=outer_up, moment=moment)


dpo_beta = 0.1
outer_rate = 0.7
outer_mu = 0.9
tiny_eps = 1e-6


def swiglu_parts(inputs, gate_w, up_w):
    gate = jnp.dot(inputs, gate_w.T, preferred_element_type=jnp.float32)
    upper = jnp.dot(inputs, up_w.T, preferred_element_type=jnp.float32)
    return gate, upper


def seq_scores(hidden, readout_rows, mask_f):
    per_token = jnp.sum(hidden.astype(jnp.float32) * readout_rows.astype(jnp.float32), axis=1)
    return jnp.sum((per_token * mask_f).reshape(SEQS, LEN), axis=1)


def dequantized(delta):
    blocks = delta.reshape(delta.shape[0], -1, BLOCK)
    scale = (jnp.max(jnp.abs(blocks), axis=2, keepdims=True) + tiny_eps).astype(jnp.bfloat16)
    levels = (blocks / scale.astype(jnp.float32)).astype(jnp.bfloat16)
    return (levels.astype(jnp.float32) * scale.astype(jnp.float32)).reshape(delta.shape)


def reference(tokens, readout, resp_mask, order, w_gate, w_up, outer_gate, outer_up, moment):
    losses = []
    grads_gate = []
    grads_up = []
    total = jnp.zeros(outer_gate.shape, jnp.float32)
    for rep_index in range(REPS):
        lower = rep_index * GROUP_TOK
        inputs = tokens[lower:lower + GROUP_TOK]
        readout_rows = readout[lower:lower + GROUP_TOK]
        mask_f = resp_mask[lower:lower + GROUP_TOK].astype(jnp.float32)
        gate, upper = swiglu_parts(inputs, w_gate[rep_index], w_up[rep_index])
        gate_ref, upper_ref = swiglu_parts(inputs, outer_gate, outer_up)
        hidden = (jax.nn.silu(gate) * upper).astype(jnp.bfloat16)
        hidden_ref = (jax.nn.silu(gate_ref) * upper_ref).astype(jnp.bfloat16)
        score = seq_scores(hidden, readout_rows, mask_f)
        score_ref = seq_scores(hidden_ref, readout_rows, mask_f)
        chosen = order[rep_index, 0::2]
        rejected = order[rep_index, 1::2]
        margin = dpo_beta * ((score[chosen] - score_ref[chosen]) - (score[rejected] - score_ref[rejected]))
        losses.append(jnp.mean(jax.nn.softplus(-margin)))
        weight = dpo_beta * jax.nn.sigmoid(-margin) / PAIRS
        coef = jnp.zeros((SEQS,), jnp.float32).at[chosen].add(-weight).at[rejected].add(weight)
        token_grad = jnp.repeat(coef, LEN) * mask_f
        hidden_grad = token_grad[:, None] * readout_rows.astype(jnp.float32)
        sigma = jax.nn.sigmoid(gate)
        gate_grad = (hidden_grad * upper * sigma * (1.0 + gate * (1.0 - sigma))).astype(jnp.bfloat16)
        up_grad = (hidden_grad * jax.nn.silu(gate)).astype(jnp.bfloat16)
        grads_gate.append(jnp.dot(gate_grad.T, inputs, preferred_element_type=jnp.float32).astype(jnp.bfloat16))
        grads_up.append(jnp.dot(up_grad.T, inputs, preferred_element_type=jnp.float32).astype(jnp.bfloat16))
        delta = outer_gate.astype(jnp.float32) - w_gate[rep_index].astype(jnp.float32)
        total = total + dequantized(delta)
    average = total / REPS
    new_moment = outer_mu * moment + average
    new_outer = (outer_gate.astype(jnp.float32) - outer_rate * (average + outer_mu * new_moment)).astype(jnp.bfloat16)
    return jnp.stack(losses), jnp.stack(grads_gate), jnp.stack(grads_up), new_outer, new_moment
```

```python
import functools

import jax
import jax.numpy as jnp
from jax import lax
from jax.experimental import pallas as pl
from jax.experimental.pallas import tpu as pltpu
from jax.sharding import PartitionSpec as P

BLOCK = 128
LEN = 16
CHUNKS = 7

dpo_beta = 0.1
outer_rate = 0.7
outer_mu = 0.9
tiny_eps = 1e-06


def project(rows, weight):
    return lax.dot_general(
        rows, weight, (((1,), (1,)), ((), ())), preferred_element_type=jnp.float32
    )


def local_scores(hidden, readout, mask_f, seqs):
    per_token = jnp.sum(hidden.astype(jnp.float32) * readout.astype(jnp.float32), axis=1)
    return jnp.sum((per_token * mask_f).reshape(seqs, LEN), axis=1)


def outer_kernel(groups, strip, me_ref, outer_ref, moment_ref, own_ref, *refs):
    del me_ref
    others = refs[: groups - 1]
    new_outer_ref, new_moment_ref = refs[-2:]
    rows, width = outer_ref.shape

    def step(index, carry):
        at = pl.ds(pl.multiple_of(index * strip, strip), strip)
        for block in range(width // BLOCK):
            cols = pl.ds(block * BLOCK, BLOCK)
            outer = outer_ref[at, cols].astype(jnp.float32)
            total = jnp.zeros_like(outer)
            for ref in (own_ref, *others):
                delta = outer - ref[at, cols].astype(jnp.float32)
                top = jnp.max(jnp.abs(delta), axis=1, keepdims=True)
                scale = (top + tiny_eps).astype(jnp.bfloat16).astype(jnp.float32)
                levels = (delta * (1.0 / scale)).astype(jnp.bfloat16)
                total = total + levels.astype(jnp.float32) * scale
            average = total * (1.0 / groups)
            new_moment = outer_mu * moment_ref[at, cols] + average
            new_moment_ref[at, cols] = new_moment
            new_outer_ref[at, cols] = (
                outer - outer_rate * (average + outer_mu * new_moment)
            ).astype(new_outer_ref.dtype)
        return carry

    lax.fori_loop(0, rows // strip, step, 0)


def outer_update(chunk, chunks, me, outer, moment, own, others, previous):
    unit_rows, width = outer.shape
    rows = unit_rows // chunks
    tile = rows
    while tile > 128 and tile % 32 == 0:
        tile //= 2
    strip = 32 if tile % 32 == 0 else 16
    first = chunk * (rows // tile)
    groups = len(others) + 1
    placed = pl.BlockSpec((tile, width), lambda i, me: (first + i, 0))
    local = pl.BlockSpec((tile, width), lambda i, me: (i, 0))
    in_specs = [
        placed,
        placed,
        pl.BlockSpec((tile, width), lambda i, me: (first + i, me[0])),
    ] + [local] * len(others)
    args = [me, outer, moment, own, *others]
    aliases = {}
    if previous is not None:
        aliases = {len(args): 0, len(args) + 1: 1}
        in_specs += [pl.BlockSpec(memory_space=pl.ANY)] * 2
        args += list(previous)
    return pl.pallas_call(
        functools.partial(outer_kernel, groups, strip),
        grid_spec=pltpu.PrefetchScalarGridSpec(
            num_scalar_prefetch=1,
            grid=(rows // tile,),
            in_specs=in_specs,
            out_specs=[placed, placed],
        ),
        out_shape=[
            jax.ShapeDtypeStruct(outer.shape, outer.dtype),
            jax.ShapeDtypeStruct(moment.shape, moment.dtype),
        ],
        input_output_aliases=aliases,
        cost_estimate=pl.CostEstimate(
            flops=rows * width * groups * 12,
            bytes_accessed=rows * width * (2 * groups + 12),
            transcendentals=0,
        ),
        name="outer_update",
    )(*args)


def per_device(tokens, readout, resp_mask, order, w_gate, w_up, outer_gate, outer_up, moment):
    groups = lax.axis_size("rep")
    me = lax.axis_index("rep")
    unit_rows, width = outer_gate.shape
    depth = tokens.shape[1]
    policy_gate = w_gate[0]
    policy_up = w_up[0]

    def swap(value, bits):
        return lax.ppermute(value, "rep", [(i, i ^ bits) for i in range(groups)])

    def columns_of(value, bits):
        return lax.dynamic_slice_in_dim(value, (me ^ bits) * width, width, 1)

    shares = [columns_of(tokens, 0)] + [
        swap(columns_of(tokens, bits), bits) for bits in range(1, groups)
    ]
    gathered = lax.all_gather(
        jnp.concatenate([tokens, *shares], axis=1), "fsdp", axis=0, tiled=True
    )
    inputs = gathered[:, :depth]
    group_tok = inputs.shape[0]

    rows = unit_rows // CHUNKS
    arrived = []
    for chunk in range(CHUNKS):
        part = policy_gate[chunk * rows : (chunk + 1) * rows]
        arrived.append([swap(columns_of(part, bits), bits) for bits in range(1, groups)])

    def reference_product(outer):
        held = [
            project(gathered[:, depth + k * width : depth + (k + 1) * width], outer)
            for k in range(groups)
        ]
        held = dict(enumerate(held))
        bit = 1
        while bit < groups:
            held = {
                k: held[k] + swap(held[k | bit].astype(jnp.bfloat16), bit).astype(jnp.float32)
                for k in held
                if not k & bit
            }
            bit *= 2
        return held[0]

    gate_ref = reference_product(outer_gate)
    upper_ref = reference_product(outer_up)
    gate = project(inputs, policy_gate)
    upper = project(inputs, policy_up)
    seqs = group_tok // LEN
    mask_f = resp_mask.astype(jnp.float32)
    hidden = (jax.nn.silu(gate) * upper).astype(jnp.bfloat16)
    hidden_ref = (jax.nn.silu(gate_ref) * upper_ref).astype(jnp.bfloat16)
    score, score_ref = lax.psum(
        (
            local_scores(hidden, readout, mask_f, seqs),
            local_scores(hidden_ref, readout, mask_f, seqs),
        ),
        "fsdp",
    )
    places = jnp.arange(seqs, dtype=jnp.int32)
    pick_chosen = (order[0, 0::2][:, None] == places[None, :]).astype(jnp.float32)
    pick_rejected = (order[0, 1::2][:, None] == places[None, :]).astype(jnp.float32)
    relative = score - score_ref
    highest = lax.Precision.HIGHEST
    margin = dpo_beta * (
        jnp.dot(pick_chosen, relative, precision=highest)
        - jnp.dot(pick_rejected, relative, precision=highest)
    )
    loss = jnp.mean(jax.nn.softplus(-margin)).reshape(1)
    weight = dpo_beta * jax.nn.sigmoid(-margin) / pick_chosen.shape[0]
    coef = jnp.dot(weight, pick_rejected - pick_chosen, precision=highest)
    token_grad = jnp.broadcast_to(coef[:, None], (seqs, LEN)).reshape(-1) * mask_f
    hidden_grad = token_grad[:, None] * readout.astype(jnp.float32)
    sigma = jax.nn.sigmoid(gate)
    gate_grad = (hidden_grad * upper * sigma * (1.0 + gate * (1.0 - sigma))).astype(jnp.bfloat16)
    up_grad = (hidden_grad * jax.nn.silu(gate)).astype(jnp.bfloat16)
    contract = (((0,), (0,)), ((), ()))
    grad_gate = lax.dot_general(
        gate_grad, inputs, contract, preferred_element_type=jnp.float32
    ).astype(jnp.bfloat16)
    grad_up = lax.dot_general(up_grad, inputs, contract, preferred_element_type=jnp.float32).astype(
        jnp.bfloat16
    )

    place = me.reshape(1).astype(jnp.int32)
    updated = None
    for chunk in range(CHUNKS):
        updated = outer_update(
            chunk, CHUNKS, place, outer_gate, moment, policy_gate, arrived[chunk], updated
        )
    new_outer, new_moment = updated
    return (loss, grad_gate[None], grad_up[None], new_outer, new_moment)


def solution(mesh):
    return jax.shard_map(
        per_device,
        mesh=mesh,
        in_specs=(
            P(("rep", "fsdp"), None),
            P("rep", "fsdp"),
            P("rep"),
            P("rep", None),
            P("rep", "fsdp", None),
            P("rep", "fsdp", None),
            P("fsdp", "rep"),
            P("fsdp", "rep"),
            P("fsdp", "rep"),
        ),
        out_specs=(
            P("rep"),
            P("rep", "fsdp", None),
            P("rep", "fsdp", None),
            P("fsdp", "rep"),
            P("fsdp", "rep"),
        ),
        check_vma=False,
    )
```

```python
import functools

import jax
import jax.numpy as jnp
from jax import lax
from jax.experimental import pallas as pl
from jax.experimental.pallas import tpu as pltpu
from jax.sharding import PartitionSpec as P

BLOCK = 128
LEN = 16
CHUNKS = 7
VMEM_LIMIT = 60 * 1024 * 1024

dpo_beta = 0.1
outer_rate = 0.7
outer_mu = 0.9
tiny_eps = 1e-06


def project(rows, weight):
    return lax.dot_general(
        rows, weight, (((1,), (1,)), ((), ())), preferred_element_type=jnp.float32
    )


def local_scores(hidden, readout, mask_f, seqs):
    per_token = jnp.sum(hidden.astype(jnp.float32) * readout.astype(jnp.float32), axis=1)
    return jnp.sum((per_token * mask_f).reshape(seqs, LEN), axis=1)


def mark(token_ref):
    token_ref[...] = jnp.zeros_like(token_ref)


TOKEN = jax.ShapeDtypeStruct((8, 128), jnp.float32)
TOKEN_SPEC = pl.BlockSpec((8, 128), lambda *_: (0, 0))
STAY = pl.BlockSpec(memory_space=pltpu.HBM)


def pick_kernel(first, width, masks, me_ref, weight_ref, *refs):
    *_, token_ref, sems = refs
    targets = refs[-2 - len(masks) : -2]
    rows = targets[0].shape[0]
    copies = []
    for index, (mask, target) in enumerate(zip(masks, targets)):
        column = pl.multiple_of((me_ref[0] ^ mask) * width, width)
        source = weight_ref.at[0, pl.ds(first, rows), pl.ds(column, width)]
        copies.append(pltpu.make_async_copy(source, target, sems.at[index]))
    for copy in copies:
        copy.start()
    mark(token_ref)
    for copy in copies:
        copy.wait()


def pick(chunk, chunks, me, weight, masks, width, *after):
    rows = weight.shape[1] // chunks
    count = len(masks)
    *parts, token = pl.pallas_call(
        functools.partial(pick_kernel, chunk * rows, width, masks),
        grid_spec=pltpu.PrefetchScalarGridSpec(
            num_scalar_prefetch=1,
            grid=(1,),
            in_specs=[STAY] * (1 + len(after)),
            out_specs=[pl.BlockSpec(memory_space=pl.ANY)] * count + [TOKEN_SPEC],
            scratch_shapes=[pltpu.SemaphoreType.DMA((count,))],
        ),
        out_shape=[jax.ShapeDtypeStruct((rows, width), weight.dtype)] * count + [TOKEN],
        cost_estimate=pl.CostEstimate(
            flops=0, bytes_accessed=rows * width * 4 * count, transcendentals=0
        ),
        compiler_params=pltpu.CompilerParams(vmem_limit_bytes=VMEM_LIMIT),
        name="pick",
    )(me, weight, *after)
    return parts, token


def assemble_kernel(groups, me_ref, tokens_ref, *refs):
    out_ref = refs[-1]
    width = out_ref.shape[2]
    for block in range(groups):
        out_ref[block] = tokens_ref[:, block * width : (block + 1) * width]
    out_ref[groups] = tokens_ref[:, pl.ds(pl.multiple_of(me_ref[0] * width, width), width)]
    for k in range(1, groups):
        out_ref[groups + k] = refs[k - 1][...]


def assemble(me, tokens, others):
    groups = len(others) + 1
    rows, depth = tokens.shape
    width = depth // groups
    whole = pl.BlockSpec((rows, width), lambda i, me: (0, 0))
    return pl.pallas_call(
        functools.partial(assemble_kernel, groups),
        grid_spec=pltpu.PrefetchScalarGridSpec(
            num_scalar_prefetch=1,
            grid=(1,),
            in_specs=[pl.BlockSpec((rows, depth), lambda i, me: (0, 0))] + [whole] * (groups - 1),
            out_specs=pl.BlockSpec((2 * groups, rows, width), lambda i, me: (0, 0, 0)),
        ),
        out_shape=jax.ShapeDtypeStruct((2 * groups, rows, width), tokens.dtype),
        compiler_params=pltpu.CompilerParams(vmem_limit_bytes=VMEM_LIMIT),
        name="assemble",
    )(me, tokens, *others)


def tile_of(rows):
    return 256 if rows % 256 == 0 else rows


def partial_kernel(shares_ref, gate_ref, up_ref, *refs):
    keep_ref, leave_ref, token_ref = refs[-3:]
    ranks, groups, rows, width = shares_ref.shape
    shares = shares_ref[...].reshape(ranks * groups * rows, width)
    mark(token_ref)
    for which, weight_ref in enumerate((gate_ref, up_ref)):
        product = project(shares, weight_ref[...])
        product = product.reshape(ranks, groups, rows, product.shape[1])
        for k in range(groups):
            part = product[:, k].reshape(ranks * rows, product.shape[3])
            if k % 2:
                leave_ref[which, k // 2] = part.astype(leave_ref.dtype)
            else:
                keep_ref[which, k // 2] = part


def partial_products(gathered, outer_gate, outer_up, *after):
    ranks, doubled, rows, width = gathered.shape
    groups = doubled // 2
    unit_rows = outer_gate.shape[0]
    tile = tile_of(unit_rows)
    group_tok = ranks * rows
    weight = pl.BlockSpec((tile, width), lambda i: (i, 0))
    result = pl.BlockSpec((2, groups // 2, group_tok, tile), lambda i: (0, 0, 0, i))
    shape = (2, groups // 2, group_tok, unit_rows)
    return pl.pallas_call(
        partial_kernel,
        grid=(unit_rows // tile,),
        in_specs=[
            pl.BlockSpec(
                (ranks, groups, rows, width),
                lambda i: (0, 1, 0, 0),
                pipeline_mode=pl.Buffered(1),
            ),
            weight,
            weight,
        ]
        + [STAY] * len(after),
        out_specs=[result, result, TOKEN_SPEC],
        out_shape=[
            jax.ShapeDtypeStruct(shape, jnp.float32),
            jax.ShapeDtypeStruct(shape, jnp.bfloat16),
            TOKEN,
        ],
        compiler_params=pltpu.CompilerParams(vmem_limit_bytes=VMEM_LIMIT),
        cost_estimate=pl.CostEstimate(
            flops=4 * groups * group_tok * width * unit_rows,
            bytes_accessed=unit_rows * (4 * width + 6 * groups * group_tok),
            transcendentals=0,
        ),
        name="partial_products",
    )(gathered, outer_gate, outer_up, *after)


def policy_kernel(blocks_ref, w_gate_ref, w_up_ref, *refs):
    gate_ref, up_ref, inputs_ref, token_ref = refs[-4:]
    ranks, groups, rows, width = blocks_ref.shape

    @pl.when(pl.program_id(0) == 0)
    def _():
        mark(token_ref)
        for block in range(groups):
            inputs_ref[:, block * width : (block + 1) * width] = blocks_ref[:, block].reshape(
                ranks * rows, width
            )

    inputs = inputs_ref[...]
    gate_ref[...] = project(inputs, w_gate_ref[0])
    up_ref[...] = project(inputs, w_up_ref[0])


def policy_products(gathered, w_gate, w_up, *after):
    ranks, doubled, rows, width = gathered.shape
    groups = doubled // 2
    unit_rows, depth = w_gate.shape[1:]
    tile = tile_of(unit_rows)
    group_tok = ranks * rows
    weight = pl.BlockSpec((1, tile, depth), lambda i: (0, i, 0))
    result = pl.BlockSpec((group_tok, tile), lambda i: (0, i))
    return pl.pallas_call(
        policy_kernel,
        grid=(unit_rows // tile,),
        in_specs=[
            pl.BlockSpec(
                (ranks, groups, rows, width),
                lambda i: (0, 0, 0, 0),
                pipeline_mode=pl.Buffered(1),
            ),
            weight,
            weight,
        ]
        + [STAY] * len(after),
        out_specs=[result, result, pl.BlockSpec((group_tok, depth), lambda i: (0, 0)), TOKEN_SPEC],
        out_shape=[
            jax.ShapeDtypeStruct((group_tok, unit_rows), jnp.float32),
            jax.ShapeDtypeStruct((group_tok, unit_rows), jnp.float32),
            jax.ShapeDtypeStruct((group_tok, depth), gathered.dtype),
            TOKEN,
        ],
        compiler_params=pltpu.CompilerParams(vmem_limit_bytes=VMEM_LIMIT),
        cost_estimate=pl.CostEstimate(
            flops=4 * group_tok * depth * unit_rows,
            bytes_accessed=unit_rows * (4 * depth + 8 * group_tok),
            transcendentals=0,
        ),
        name="policy_products",
    )(gathered, w_gate, w_up, *after)


def outer_kernel(groups, strip, me_ref, outer_ref, moment_ref, *refs):
    del me_ref
    inner = refs[:groups]
    new_outer_ref, new_moment_ref, token_ref = refs[-3:]
    rows, width = outer_ref.shape
    mark(token_ref)

    def step(index, carry):
        at = pl.ds(pl.multiple_of(index * strip, strip), strip)
        for block in range(width // BLOCK):
            cols = pl.ds(block * BLOCK, BLOCK)
            outer = outer_ref[at, cols].astype(jnp.float32)
            total = jnp.zeros_like(outer)
            for ref in inner:
                delta = outer - ref[at, cols].astype(jnp.float32)
                top = jnp.max(jnp.abs(delta), axis=1, keepdims=True)
                scale = (top + tiny_eps).astype(jnp.bfloat16).astype(jnp.float32)
                levels = (delta * (1.0 / scale)).astype(jnp.bfloat16)
                total = total + levels.astype(jnp.float32) * scale
            average = total * (1.0 / groups)
            new_moment = outer_mu * moment_ref[at, cols] + average
            new_moment_ref[at, cols] = new_moment
            new_outer_ref[at, cols] = (
                outer - outer_rate * (average + outer_mu * new_moment)
            ).astype(new_outer_ref.dtype)
        return carry

    lax.fori_loop(0, rows // strip, step, 0)


def outer_update(chunk, chunks, me, outer, moment, near, far, previous, *after):
    unit_rows, width = outer.shape
    rows = unit_rows // chunks
    tile = rows // 2 if rows % 64 == 0 else rows
    strip = 32 if tile % 32 == 0 else 16
    first = chunk * (rows // tile)
    groups = len(near) + len(far)
    placed = pl.BlockSpec((tile, width), lambda i, me: (first + i, 0))
    local = pl.BlockSpec((tile, width), lambda i, me: (i, 0))
    in_specs = [placed] * (2 + len(near)) + [local] * len(far)
    args = [me, outer, moment, *near, *far]
    aliases = {}
    if previous is not None:
        aliases = {len(args): 0, len(args) + 1: 1}
        in_specs += [STAY] * 2
        args += list(previous)
    in_specs += [STAY] * len(after)
    args += list(after)
    *updated, token = pl.pallas_call(
        functools.partial(outer_kernel, groups, strip),
        grid_spec=pltpu.PrefetchScalarGridSpec(
            num_scalar_prefetch=1,
            grid=(rows // tile,),
            in_specs=in_specs,
            out_specs=[placed, placed, TOKEN_SPEC],
        ),
        out_shape=[
            jax.ShapeDtypeStruct(outer.shape, outer.dtype),
            jax.ShapeDtypeStruct(moment.shape, moment.dtype),
            TOKEN,
        ],
        input_output_aliases=aliases,
        cost_estimate=pl.CostEstimate(
            flops=rows * width * groups * 12,
            bytes_accessed=rows * width * (2 * groups + 12),
            transcendentals=0,
        ),
        compiler_params=pltpu.CompilerParams(vmem_limit_bytes=VMEM_LIMIT),
        name="outer_update",
    )(*args)
    return updated, token


def per_device(tokens, readout, resp_mask, order, w_gate, w_up, outer_gate, outer_up, moment):
    groups = lax.axis_size("rep")
    ranks = lax.axis_size("fsdp")
    place = lax.axis_index("rep").reshape(1).astype(jnp.int32)
    width = outer_gate.shape[1]

    def swap(value, bits):
        return lax.ppermute(value, "rep", [(i, i ^ bits) for i in range(groups)])

    far_masks = tuple(range(2, groups))

    def send(chunk, *after):
        parts, token = pick(chunk, CHUNKS, place, w_gate, far_masks, width, *after)
        return [swap(part, bits) for part, bits in zip(parts, far_masks)], token

    far = [None] * CHUNKS
    updated = None

    def update(chunk, *after):
        return outer_update(
            chunk, CHUNKS, place, outer_gate, moment, near, far[chunk], updated, *after
        )

    shares, token = pick(0, 1, place, tokens[None], tuple(range(1, groups)), width)
    others = [swap(share, bits) for bits, share in enumerate(shares, 1)]
    far[0], token = send(0, token)
    far[1], token = send(1, token)
    gathered = lax.all_gather(assemble(place, tokens, others), "fsdp", axis=0, tiled=False)
    (own, mate), token = pick(0, 1, place, w_gate, (0, 1), width, token)
    near = [own, swap(mate, 1)]

    updated, token = update(0)
    far[2], token = send(2, token)
    updated, token = update(1, token)
    far[3], token = send(3, token)

    keep, leave, token = partial_products(gathered, outer_gate, outer_up, token)
    held = keep + swap(leave, 1).astype(jnp.float32)
    leaving = held[:, 1].astype(jnp.bfloat16)
    both_ref = held[:, 0] + swap(leaving, 2).astype(jnp.float32)
    gate_ref, upper_ref = both_ref[0], both_ref[1]

    gate, upper, inputs, token = policy_products(gathered, w_gate, w_up, leaving)
    updated, token = update(2, token)
    far[4], token = send(4, token)
    updated, token = update(3, token)
    far[5], token = send(5, token)

    group_tok = inputs.shape[0]
    seqs = group_tok // LEN
    mask_f = resp_mask.astype(jnp.float32)
    hidden = (jax.nn.silu(gate) * upper).astype(jnp.bfloat16)
    hidden_ref = (jax.nn.silu(gate_ref) * upper_ref).astype(jnp.bfloat16)
    relative = local_scores(hidden, readout, mask_f, seqs) - local_scores(
        hidden_ref, readout, mask_f, seqs
    )
    hop = 1
    while hop < ranks:
        relative = relative + lax.ppermute(
            relative, "fsdp", [(i, i ^ hop) for i in range(ranks)]
        )
        hop *= 2
    places = jnp.arange(seqs, dtype=jnp.int32)
    pick_chosen = (order[0, 0::2][:, None] == places[None, :]).astype(jnp.float32)
    pick_rejected = (order[0, 1::2][:, None] == places[None, :]).astype(jnp.float32)
    highest = lax.Precision.HIGHEST
    margin = dpo_beta * (
        jnp.dot(pick_chosen, relative, precision=highest)
        - jnp.dot(pick_rejected, relative, precision=highest)
    )
    loss = jnp.mean(jax.nn.softplus(-margin)).reshape(1)
    weight = dpo_beta * jax.nn.sigmoid(-margin) / pick_chosen.shape[0]
    coef = jnp.dot(weight, pick_rejected - pick_chosen, precision=highest)
    token_grad = jnp.broadcast_to(coef[:, None], (seqs, LEN)).reshape(-1) * mask_f
    hidden_grad = token_grad[:, None] * readout.astype(jnp.float32)
    sigma = jax.nn.sigmoid(gate)
    gate_grad = (hidden_grad * upper * sigma * (1.0 + gate * (1.0 - sigma))).astype(jnp.bfloat16)
    up_grad = (hidden_grad * jax.nn.silu(gate)).astype(jnp.bfloat16)
    contract = (((0,), (0,)), ((), ()))
    grad_gate = lax.dot_general(
        gate_grad, inputs, contract, preferred_element_type=jnp.float32
    ).astype(jnp.bfloat16)
    grad_up = lax.dot_general(up_grad, inputs, contract, preferred_element_type=jnp.float32).astype(
        jnp.bfloat16
    )

    updated, token = update(4, token, grad_gate)
    far[6], token = send(6, token)
    updated, token = update(5, token, grad_up)
    updated, token = update(6, token)
    new_outer, new_moment = updated
    return (loss, grad_gate[None], grad_up[None], new_outer, new_moment)


def solution(mesh):
    return jax.shard_map(
        per_device,
        mesh=mesh,
        in_specs=(
            P(("rep", "fsdp"), None),
            P("rep", "fsdp"),
            P("rep"),
            P("rep", None),
            P("rep", "fsdp", None),
            P("rep", "fsdp", None),
            P("fsdp", "rep"),
            P("fsdp", "rep"),
            P("fsdp", "rep"),
        ),
        out_specs=(
            P("rep"),
            P("rep", "fsdp", None),
            P("rep", "fsdp", None),
            P("fsdp", "rep"),
            P("fsdp", "rep"),
        ),
        check_vma=False,
    )
```

```python
import functools

import jax
import jax.numpy as jnp
from jax import lax
from jax.experimental import pallas as pl
from jax.experimental.pallas import tpu as pltpu
from jax.sharding import PartitionSpec as P

BLOCK = 128
LEN = 16
CHUNKS = 7
VMEM_LIMIT = 60 * 1024 * 1024

dpo_beta = 0.1
outer_rate = 0.7
outer_mu = 0.9
tiny_eps = 1e-06


def project(rows, weight):
    return lax.dot_general(
        rows, weight, (((1,), (1,)), ((), ())), preferred_element_type=jnp.float32
    )


def local_scores(hidden, readout, mask_f, seqs):
    per_token = jnp.sum(hidden.astype(jnp.float32) * readout.astype(jnp.float32), axis=1)
    return jnp.sum((per_token * mask_f).reshape(seqs, LEN), axis=1)


def tile_of(rows):
    return 256 if rows % 256 == 0 else rows


def mark(token_ref):
    token_ref[...] = jnp.zeros_like(token_ref)


TOKEN = jax.ShapeDtypeStruct((8, 128), jnp.float32)
TOKEN_SPEC = pl.BlockSpec((8, 128), lambda *_: (0, 0))
STAY = pl.BlockSpec(memory_space=pltpu.HBM)


def pick_kernel(count, me_ref, *refs):
    del me_ref
    token_ref = refs[-1]
    mark(token_ref)
    for source_ref, target_ref in zip(refs[:count], refs[-1 - count : -1]):
        target_ref[...] = source_ref[0]


def pick(chunk, chunks, me, weight, masks, width, *after):
    rows = weight.shape[1] // chunks
    tile = tile_of(rows)
    first = chunk * (rows // tile)
    count = len(masks)
    *parts, token = pl.pallas_call(
        functools.partial(pick_kernel, count),
        grid_spec=pltpu.PrefetchScalarGridSpec(
            num_scalar_prefetch=1,
            grid=(rows // tile,),
            in_specs=[
                pl.BlockSpec(
                    (1, tile, width), lambda i, me, mask=mask: (0, first + i, me[0] ^ mask)
                )
                for mask in masks
            ]
            + [STAY] * len(after),
            out_specs=[pl.BlockSpec((tile, width), lambda i, me: (i, 0))] * count + [TOKEN_SPEC],
        ),
        out_shape=[jax.ShapeDtypeStruct((rows, width), weight.dtype)] * count + [TOKEN],
        cost_estimate=pl.CostEstimate(
            flops=0, bytes_accessed=rows * width * 4 * count, transcendentals=0
        ),
        compiler_params=pltpu.CompilerParams(vmem_limit_bytes=VMEM_LIMIT),
        name="pick",
    )(me, *[weight] * count, *after)
    return parts, token


def assemble_kernel(groups, me_ref, tokens_ref, *refs):
    out_ref = refs[-1]
    width = out_ref.shape[2]
    for block in range(groups):
        out_ref[block] = tokens_ref[:, block * width : (block + 1) * width]
    out_ref[groups] = tokens_ref[:, pl.ds(pl.multiple_of(me_ref[0] * width, width), width)]
    for k in range(1, groups):
        out_ref[groups + k] = refs[k - 1][...]


def assemble(me, tokens, others):
    groups = len(others) + 1
    rows, depth = tokens.shape
    width = depth // groups
    whole = pl.BlockSpec((rows, width), lambda i, me: (0, 0))
    return pl.pallas_call(
        functools.partial(assemble_kernel, groups),
        grid_spec=pltpu.PrefetchScalarGridSpec(
            num_scalar_prefetch=1,
            grid=(1,),
            in_specs=[pl.BlockSpec((rows, depth), lambda i, me: (0, 0))] + [whole] * (groups - 1),
            out_specs=pl.BlockSpec((2 * groups, rows, width), lambda i, me: (0, 0, 0)),
        ),
        out_shape=jax.ShapeDtypeStruct((2 * groups, rows, width), tokens.dtype),
        compiler_params=pltpu.CompilerParams(vmem_limit_bytes=VMEM_LIMIT),
        name="assemble",
    )(me, tokens, *others)


def partial_kernel(shares_ref, gate_ref, up_ref, *refs):
    keep_ref, leave_ref, token_ref = refs[-3:]
    ranks, groups, rows, width = shares_ref.shape
    shares = shares_ref[...].reshape(ranks * groups * rows, width)
    mark(token_ref)
    for which, weight_ref in enumerate((gate_ref, up_ref)):
        product = project(shares, weight_ref[...])
        product = product.reshape(ranks, groups, rows, product.shape[1])
        for k in range(groups):
            part = product[:, k].reshape(ranks * rows, product.shape[3])
            if k % 2:
                leave_ref[which, k // 2] = part.astype(leave_ref.dtype)
            else:
                keep_ref[which, k // 2] = part


def partial_products(gathered, outer_gate, outer_up, *after):
    ranks, doubled, rows, width = gathered.shape
    groups = doubled // 2
    unit_rows = outer_gate.shape[0]
    tile = tile_of(unit_rows)
    group_tok = ranks * rows
    weight = pl.BlockSpec((tile, width), lambda i: (i, 0))
    result = pl.BlockSpec((2, groups // 2, group_tok, tile), lambda i: (0, 0, 0, i))
    shape = (2, groups // 2, group_tok, unit_rows)
    return pl.pallas_call(
        partial_kernel,
        grid=(unit_rows // tile,),
        in_specs=[
            pl.BlockSpec(
                (ranks, groups, rows, width),
                lambda i: (0, 1, 0, 0),
                pipeline_mode=pl.Buffered(1),
            ),
            weight,
            weight,
        ]
        + [STAY] * len(after),
        out_specs=[result, result, TOKEN_SPEC],
        out_shape=[
            jax.ShapeDtypeStruct(shape, jnp.float32),
            jax.ShapeDtypeStruct(shape, jnp.bfloat16),
            TOKEN,
        ],
        compiler_params=pltpu.CompilerParams(vmem_limit_bytes=VMEM_LIMIT),
        cost_estimate=pl.CostEstimate(
            flops=4 * groups * group_tok * width * unit_rows,
            bytes_accessed=unit_rows * (4 * width + 6 * groups * group_tok),
            transcendentals=0,
        ),
        name="partial_products",
    )(gathered, outer_gate, outer_up, *after)


def policy_kernel(blocks_ref, w_gate_ref, w_up_ref, *refs):
    gate_ref, up_ref, inputs_ref, token_ref = refs[-4:]
    ranks, groups, rows, width = blocks_ref.shape

    @pl.when(pl.program_id(0) == 0)
    def _():
        mark(token_ref)
        for block in range(groups):
            inputs_ref[:, block * width : (block + 1) * width] = blocks_ref[:, block].reshape(
                ranks * rows, width
            )

    inputs = inputs_ref[...]
    gate_ref[...] = project(inputs, w_gate_ref[0])
    up_ref[...] = project(inputs, w_up_ref[0])


def policy_products(gathered, w_gate, w_up, *after):
    ranks, doubled, rows, width = gathered.shape
    groups = doubled // 2
    unit_rows, depth = w_gate.shape[1:]
    tile = tile_of(unit_rows)
    group_tok = ranks * rows
    weight = pl.BlockSpec((1, tile, depth), lambda i: (0, i, 0))
    result = pl.BlockSpec((group_tok, tile), lambda i: (0, i))
    return pl.pallas_call(
        policy_kernel,
        grid=(unit_rows // tile,),
        in_specs=[
            pl.BlockSpec(
                (ranks, groups, rows, width),
                lambda i: (0, 0, 0, 0),
                pipeline_mode=pl.Buffered(1),
            ),
            weight,
            weight,
        ]
        + [STAY] * len(after),
        out_specs=[result, result, pl.BlockSpec((group_tok, depth), lambda i: (0, 0)), TOKEN_SPEC],
        out_shape=[
            jax.ShapeDtypeStruct((group_tok, unit_rows), jnp.float32),
            jax.ShapeDtypeStruct((group_tok, unit_rows), jnp.float32),
            jax.ShapeDtypeStruct((group_tok, depth), gathered.dtype),
            TOKEN,
        ],
        compiler_params=pltpu.CompilerParams(vmem_limit_bytes=VMEM_LIMIT),
        cost_estimate=pl.CostEstimate(
            flops=4 * group_tok * depth * unit_rows,
            bytes_accessed=unit_rows * (4 * depth + 8 * group_tok),
            transcendentals=0,
        ),
        name="policy_products",
    )(gathered, w_gate, w_up, *after)


def outer_kernel(groups, strip, me_ref, outer_ref, moment_ref, *refs):
    del me_ref
    inner = refs[:groups]
    new_outer_ref, new_moment_ref, token_ref = refs[-3:]
    rows, width = outer_ref.shape
    mark(token_ref)

    def step(index, carry):
        at = pl.ds(pl.multiple_of(index * strip, strip), strip)
        for block in range(width // BLOCK):
            cols = pl.ds(block * BLOCK, BLOCK)
            outer = outer_ref[at, cols].astype(jnp.float32)
            total = jnp.zeros_like(outer)
            for ref in inner:
                delta = outer - ref[at, cols].astype(jnp.float32)
                top = jnp.max(jnp.abs(delta), axis=1, keepdims=True)
                scale = (top + tiny_eps).astype(jnp.bfloat16).astype(jnp.float32)
                levels = (delta * (1.0 / scale)).astype(jnp.bfloat16)
                total = total + levels.astype(jnp.float32) * scale
            average = total * (1.0 / groups)
            new_moment = outer_mu * moment_ref[at, cols] + average
            new_moment_ref[at, cols] = new_moment
            new_outer_ref[at, cols] = (
                outer - outer_rate * (average + outer_mu * new_moment)
            ).astype(new_outer_ref.dtype)
        return carry

    lax.fori_loop(0, rows // strip, step, 0)


def outer_update(chunk, chunks, me, outer, moment, near, far, previous, *after):
    unit_rows, width = outer.shape
    rows = unit_rows // chunks
    tile = rows // 2 if rows % 64 == 0 else rows
    strip = 32 if tile % 32 == 0 else 16
    first = chunk * (rows // tile)
    groups = len(near) + len(far)
    placed = pl.BlockSpec((tile, width), lambda i, me: (first + i, 0))
    local = pl.BlockSpec((tile, width), lambda i, me: (i, 0))
    in_specs = [placed] * (2 + len(near)) + [local] * len(far)
    args = [me, outer, moment, *near, *far]
    aliases = {}
    if previous is not None:
        aliases = {len(args): 0, len(args) + 1: 1}
        in_specs += [STAY] * 2
        args += list(previous)
    in_specs += [STAY] * len(after)
    args += list(after)
    *updated, token = pl.pallas_call(
        functools.partial(outer_kernel, groups, strip),
        grid_spec=pltpu.PrefetchScalarGridSpec(
            num_scalar_prefetch=1,
            grid=(rows // tile,),
            in_specs=in_specs,
            out_specs=[placed, placed, TOKEN_SPEC],
        ),
        out_shape=[
            jax.ShapeDtypeStruct(outer.shape, outer.dtype),
            jax.ShapeDtypeStruct(moment.shape, moment.dtype),
            TOKEN,
        ],
        input_output_aliases=aliases,
        cost_estimate=pl.CostEstimate(
            flops=rows * width * groups * 12,
            bytes_accessed=rows * width * (2 * groups + 12),
            transcendentals=0,
        ),
        compiler_params=pltpu.CompilerParams(vmem_limit_bytes=VMEM_LIMIT),
        name="outer_update",
    )(*args)
    return updated, token


def per_device(tokens, readout, resp_mask, order, w_gate, w_up, outer_gate, outer_up, moment):
    groups = lax.axis_size("rep")
    ranks = lax.axis_size("fsdp")
    place = lax.axis_index("rep").reshape(1).astype(jnp.int32)
    width = outer_gate.shape[1]

    def swap(value, bits):
        return lax.ppermute(value, "rep", [(i, i ^ bits) for i in range(groups)])

    far_masks = tuple(range(2, groups))

    def send(chunk, *after):
        parts, token = pick(chunk, CHUNKS, place, w_gate, far_masks, width, *after)
        return [swap(part, bits) for part, bits in zip(parts, far_masks)], token

    far = [None] * CHUNKS
    updated = None

    def update(chunk, *after):
        return outer_update(
            chunk, CHUNKS, place, outer_gate, moment, near, far[chunk], updated, *after
        )

    shares, token = pick(0, 1, place, tokens[None], tuple(range(1, groups)), width)
    others = [swap(share, bits) for bits, share in enumerate(shares, 1)]
    far[0], token = send(0, token)
    far[1], token = send(1, token)
    gathered = lax.all_gather(assemble(place, tokens, others), "fsdp", axis=0, tiled=False)
    (own, mate), token = pick(0, 1, place, w_gate, (0, 1), width, token)
    near = [own, swap(mate, 1)]

    updated, token = update(0)
    far[2], token = send(2, token)
    updated, token = update(1, token)
    far[3], token = send(3, token)

    keep, leave, token = partial_products(gathered, outer_gate, outer_up, token)
    held = keep + swap(leave, 1).astype(jnp.float32)
    leaving = held[:, 1].astype(jnp.bfloat16)
    both_ref = held[:, 0] + swap(leaving, 2).astype(jnp.float32)
    gate_ref, upper_ref = both_ref[0], both_ref[1]

    gate, upper, inputs, token = policy_products(gathered, w_gate, w_up, leaving)
    updated, token = update(2, token)
    far[4], token = send(4, token)
    updated, token = update(3, token)
    far[5], token = send(5, token)

    group_tok = inputs.shape[0]
    seqs = group_tok // LEN
    mask_f = resp_mask.astype(jnp.float32)
    hidden = (jax.nn.silu(gate) * upper).astype(jnp.bfloat16)
    hidden_ref = (jax.nn.silu(gate_ref) * upper_ref).astype(jnp.bfloat16)
    relative = local_scores(hidden, readout, mask_f, seqs) - local_scores(
        hidden_ref, readout, mask_f, seqs
    )
    hop = 1
    while hop < ranks:
        relative = relative + lax.ppermute(
            relative, "fsdp", [(i, i ^ hop) for i in range(ranks)]
        )
        hop *= 2
    places = jnp.arange(seqs, dtype=jnp.int32)
    pick_chosen = (order[0, 0::2][:, None] == places[None, :]).astype(jnp.float32)
    pick_rejected = (order[0, 1::2][:, None] == places[None, :]).astype(jnp.float32)
    highest = lax.Precision.HIGHEST
    margin = dpo_beta * (
        jnp.dot(pick_chosen, relative, precision=highest)
        - jnp.dot(pick_rejected, relative, precision=highest)
    )
    loss = jnp.mean(jax.nn.softplus(-margin)).reshape(1)
    weight = dpo_beta * jax.nn.sigmoid(-margin) / pick_chosen.shape[0]
    coef = jnp.dot(weight, pick_rejected - pick_chosen, precision=highest)
    token_grad = jnp.broadcast_to(coef[:, None], (seqs, LEN)).reshape(-1) * mask_f
    hidden_grad = token_grad[:, None] * readout.astype(jnp.float32)
    sigma = jax.nn.sigmoid(gate)
    gate_grad = (hidden_grad * upper * sigma * (1.0 + gate * (1.0 - sigma))).astype(jnp.bfloat16)
    up_grad = (hidden_grad * jax.nn.silu(gate)).astype(jnp.bfloat16)
    contract = (((0,), (0,)), ((), ()))
    grad_gate = lax.dot_general(
        gate_grad, inputs, contract, preferred_element_type=jnp.float32
    ).astype(jnp.bfloat16)
    grad_up = lax.dot_general(up_grad, inputs, contract, preferred_element_type=jnp.float32).astype(
        jnp.bfloat16
    )

    updated, token = update(4, token, grad_gate)
    far[6], token = send(6, token)
    updated, token = update(5, token, grad_up)
    updated, token = update(6, token)
    new_outer, new_moment = updated
    return (loss, grad_gate[None], grad_up[None], new_outer, new_moment)


def solution(mesh):
    return jax.shard_map(
        per_device,
        mesh=mesh,
        in_specs=(
            P(("rep", "fsdp"), None),
            P("rep", "fsdp"),
            P("rep"),
            P("rep", None),
            P("rep", "fsdp", None),
            P("rep", "fsdp", None),
            P("fsdp", "rep"),
            P("fsdp", "rep"),
            P("fsdp", "rep"),
        ),
        out_specs=(
            P("rep"),
            P("rep", "fsdp", None),
            P("rep", "fsdp", None),
            P("fsdp", "rep"),
            P("fsdp", "rep"),
        ),
        check_vma=False,
    )
```

```python
import functools

import jax
import jax.numpy as jnp
from jax import lax
from jax.experimental import pallas as pl
from jax.experimental.pallas import tpu as pltpu
from jax.sharding import PartitionSpec as P

BLOCK = 128
LEN = 16
CHUNKS = (4, 5, 3, 1, 1)
VMEM_LIMIT = 60 * 1024 * 1024
BRIEF = pl.CostEstimate(flops=1, bytes_accessed=1, transcendentals=0)

dpo_beta = 0.1
outer_rate = 0.7
outer_mu = 0.9
tiny_eps = 1e-06


def project(rows, weight):
    return lax.dot_general(
        rows, weight, (((1,), (1,)), ((), ())), preferred_element_type=jnp.float32
    )


def local_scores(hidden, readout, mask_f, seqs):
    per_token = jnp.sum(hidden.astype(jnp.float32) * readout.astype(jnp.float32), axis=1)
    return jnp.sum((per_token * mask_f).reshape(seqs, LEN), axis=1)


def tile_of(rows):
    return 256 if rows % 256 == 0 else rows


def mark(token_ref):
    token_ref[...] = jnp.zeros_like(token_ref)


TOKEN = jax.ShapeDtypeStruct((8, 128), jnp.float32)
TOKEN_SPEC = pl.BlockSpec((8, 128), lambda *_: (0, 0))
STAY = pl.BlockSpec(memory_space=pltpu.HBM)


def pick_kernel(count, me_ref, *refs):
    del me_ref
    token_ref = refs[-1]
    mark(token_ref)
    for source_ref, target_ref in zip(refs[:count], refs[-1 - count : -1]):
        target_ref[...] = source_ref[0]


def pick(first, steps, tile, me, weight, masks, width, *after):
    rows = steps * tile
    count = len(masks)
    *parts, token = pl.pallas_call(
        functools.partial(pick_kernel, count),
        grid_spec=pltpu.PrefetchScalarGridSpec(
            num_scalar_prefetch=1,
            grid=(steps,),
            in_specs=[
                pl.BlockSpec(
                    (1, tile, width), lambda i, me, mask=mask: (0, first + i, me[0] ^ mask)
                )
                for mask in masks
            ]
            + [STAY] * len(after),
            out_specs=[pl.BlockSpec((tile, width), lambda i, me: (i, 0))] * count + [TOKEN_SPEC],
        ),
        out_shape=[jax.ShapeDtypeStruct((rows, width), weight.dtype)] * count + [TOKEN],
        cost_estimate=BRIEF,
        compiler_params=pltpu.CompilerParams(vmem_limit_bytes=VMEM_LIMIT),
        name="pick",
    )(me, *[weight] * count, *after)
    return parts, token


def assemble_kernel(groups, me_ref, tokens_ref, *refs):
    out_ref, token_ref = refs[-2:]
    width = out_ref.shape[2]
    mark(token_ref)
    for block in range(groups):
        out_ref[block] = tokens_ref[:, block * width : (block + 1) * width]
    out_ref[groups] = tokens_ref[:, pl.ds(pl.multiple_of(me_ref[0] * width, width), width)]
    for k in range(1, groups):
        out_ref[groups + k] = refs[k - 1][...]


def assemble(me, tokens, others, *after):
    groups = len(others) + 1
    rows, depth = tokens.shape
    width = depth // groups
    whole = pl.BlockSpec((rows, width), lambda i, me: (0, 0))
    return pl.pallas_call(
        functools.partial(assemble_kernel, groups),
        grid_spec=pltpu.PrefetchScalarGridSpec(
            num_scalar_prefetch=1,
            grid=(1,),
            in_specs=[pl.BlockSpec((rows, depth), lambda i, me: (0, 0))] + [whole] * (groups - 1)
            + [STAY] * len(after),
            out_specs=[
                pl.BlockSpec((2 * groups, rows, width), lambda i, me: (0, 0, 0)),
                TOKEN_SPEC,
            ],
        ),
        out_shape=[jax.ShapeDtypeStruct((2 * groups, rows, width), tokens.dtype), TOKEN],
        cost_estimate=BRIEF,
        compiler_params=pltpu.CompilerParams(vmem_limit_bytes=VMEM_LIMIT),
        name="assemble",
    )(me, tokens, *others, *after)


def partial_kernel(shares_ref, gate_ref, up_ref, *refs):
    *results, token_ref = refs[-1 - 2 * shares_ref.shape[1] :]
    ranks, groups, rows, width = shares_ref.shape
    shares = shares_ref[...].reshape(ranks * groups * rows, width)
    mark(token_ref)
    for which, weight_ref in enumerate((gate_ref, up_ref)):
        product = project(shares, weight_ref[...])
        product = product.reshape(ranks, groups, rows, product.shape[1])
        for k in range(groups):
            part = product[:, k].reshape(ranks * rows, product.shape[3])
            target_ref = results[which * groups + k]
            target_ref[...] = part.astype(target_ref.dtype)


def partial_products(gathered, outer_gate, outer_up, *after):
    ranks, doubled, rows, width = gathered.shape
    groups = doubled // 2
    unit_rows = outer_gate.shape[0]
    tile = tile_of(unit_rows)
    group_tok = ranks * rows
    weight = pl.BlockSpec((tile, width), lambda i: (i, 0))
    result = pl.BlockSpec((group_tok, tile), lambda i: (0, i))
    return pl.pallas_call(
        partial_kernel,
        grid=(unit_rows // tile,),
        in_specs=[
            pl.BlockSpec(
                (ranks, groups, rows, width),
                lambda i: (0, 1, 0, 0),
                pipeline_mode=pl.Buffered(1),
            ),
            weight,
            weight,
        ]
        + [STAY] * len(after),
        out_specs=[result] * (2 * groups) + [TOKEN_SPEC],
        out_shape=[
            jax.ShapeDtypeStruct(
                (group_tok, unit_rows), jnp.bfloat16 if k % 2 else jnp.float32
            )
            for _ in range(2)
            for k in range(groups)
        ]
        + [TOKEN],
        compiler_params=pltpu.CompilerParams(vmem_limit_bytes=VMEM_LIMIT),
        cost_estimate=BRIEF,
        name="partial_products",
    )(gathered, outer_gate, outer_up, *after)


def join_kernel(*refs):
    *parts, leave_gate_ref, leave_up_ref, stay_gate_ref, stay_up_ref, token_ref = refs
    mark(token_ref)
    targets = ((leave_gate_ref, stay_gate_ref), (leave_up_ref, stay_up_ref))
    for which, (leave_ref, target_ref) in enumerate(targets):
        stay_ref, mate_ref, far_ref, both_ref = parts[4 * which : 4 * which + 4]
        target_ref[...] = stay_ref[...] + mate_ref[...].astype(jnp.float32)
        leave_ref[...] = (far_ref[...] + both_ref[...].astype(jnp.float32)).astype(
            leave_ref.dtype
        )


def join(parts):
    group_tok, unit_rows = parts[0].shape
    tile = tile_of(unit_rows)
    block = pl.BlockSpec((group_tok, tile), lambda i: (0, i))
    leave = jax.ShapeDtypeStruct((group_tok, unit_rows), jnp.bfloat16)
    stay = jax.ShapeDtypeStruct((group_tok, unit_rows), jnp.float32)
    return pl.pallas_call(
        join_kernel,
        grid=(unit_rows // tile,),
        in_specs=[block] * len(parts),
        out_specs=[block] * 4 + [TOKEN_SPEC],
        out_shape=[leave, leave, stay, stay, TOKEN],
        compiler_params=pltpu.CompilerParams(vmem_limit_bytes=VMEM_LIMIT),
        cost_estimate=BRIEF,
        name="join",
    )(*parts)


def policy_kernel(blocks_ref, w_gate_ref, w_up_ref, *refs):
    gate_ref, up_ref, inputs_ref, token_ref = refs[-4:]
    ranks, groups, rows, width = blocks_ref.shape

    @pl.when(pl.program_id(0) == 0)
    def _():
        mark(token_ref)
        for block in range(groups):
            inputs_ref[:, block * width : (block + 1) * width] = blocks_ref[:, block].reshape(
                ranks * rows, width
            )

    inputs = inputs_ref[...]
    gate_ref[...] = project(inputs, w_gate_ref[0])
    up_ref[...] = project(inputs, w_up_ref[0])


def policy_products(gathered, w_gate, w_up, *after):
    ranks, doubled, rows, width = gathered.shape
    groups = doubled // 2
    unit_rows, depth = w_gate.shape[1:]
    tile = tile_of(unit_rows)
    group_tok = ranks * rows
    weight = pl.BlockSpec((1, tile, depth), lambda i: (0, i, 0))
    result = pl.BlockSpec((group_tok, tile), lambda i: (0, i))
    return pl.pallas_call(
        policy_kernel,
        grid=(unit_rows // tile,),
        in_specs=[
            pl.BlockSpec(
                (ranks, groups, rows, width),
                lambda i: (0, 0, 0, 0),
                pipeline_mode=pl.Buffered(1),
            ),
            weight,
            weight,
        ]
        + [STAY] * len(after),
        out_specs=[result, result, pl.BlockSpec((group_tok, depth), lambda i: (0, 0)), TOKEN_SPEC],
        out_shape=[
            jax.ShapeDtypeStruct((group_tok, unit_rows), jnp.float32),
            jax.ShapeDtypeStruct((group_tok, unit_rows), jnp.float32),
            jax.ShapeDtypeStruct((group_tok, depth), gathered.dtype),
            TOKEN,
        ],
        compiler_params=pltpu.CompilerParams(vmem_limit_bytes=VMEM_LIMIT),
        cost_estimate=BRIEF,
        name="policy_products",
    )(gathered, w_gate, w_up, *after)


def grads_kernel(gate_ref, up_ref, readout_ref, token_grad_ref, inputs_ref, *refs):
    grad_gate_ref, grad_up_ref, token_ref = refs[-3:]
    mark(token_ref)
    gate = gate_ref[...]
    hidden_grad = token_grad_ref[...] * readout_ref[...].astype(jnp.float32)
    sigma = jax.nn.sigmoid(gate)
    gate_grad = hidden_grad * up_ref[...] * sigma * (1.0 + gate * (1.0 - sigma))
    up_grad = hidden_grad * (gate * sigma)
    contract = (((0,), (0,)), ((), ()))
    for target_ref, grad in ((grad_gate_ref, gate_grad), (grad_up_ref, up_grad)):
        target_ref[0] = lax.dot_general(
            grad.astype(jnp.bfloat16),
            inputs_ref[...],
            contract,
            preferred_element_type=jnp.float32,
        ).astype(target_ref.dtype)


def weight_grads(gate, upper, readout, token_grad, inputs, *after):
    group_tok, unit_rows = gate.shape
    depth = inputs.shape[1]
    tile = tile_of(unit_rows)
    units = pl.BlockSpec((group_tok, tile), lambda i: (0, i))
    result = pl.BlockSpec((1, tile, depth), lambda i: (0, i, 0))
    shape = jax.ShapeDtypeStruct((1, unit_rows, depth), jnp.bfloat16)
    return pl.pallas_call(
        grads_kernel,
        grid=(unit_rows // tile,),
        in_specs=[
            units,
            units,
            units,
            pl.BlockSpec((group_tok, 1), lambda i: (0, 0)),
            pl.BlockSpec(
                (group_tok, depth), lambda i: (0, 0), pipeline_mode=pl.Buffered(1)
            ),
        ]
        + [STAY] * len(after),
        out_specs=[result, result, TOKEN_SPEC],
        out_shape=[shape, shape, TOKEN],
        compiler_params=pltpu.CompilerParams(vmem_limit_bytes=VMEM_LIMIT),
        cost_estimate=BRIEF,
        name="weight_grads",
    )(gate, upper, readout, token_grad[:, None], inputs, *after)


def outer_kernel(groups, strip, me_ref, outer_ref, moment_ref, *refs):
    del me_ref
    inner = (refs[0].at[0], *refs[1:groups])
    new_outer_ref, new_moment_ref, token_ref = refs[-3:]
    rows, width = outer_ref.shape
    mark(token_ref)

    def step(index, carry):
        at = pl.ds(pl.multiple_of(index * strip, strip), strip)
        for block in range(width // BLOCK):
            cols = pl.ds(block * BLOCK, BLOCK)
            outer = outer_ref[at, cols].astype(jnp.float32)
            total = jnp.zeros_like(outer)
            for ref in inner:
                delta = outer - ref[at, cols].astype(jnp.float32)
                top = jnp.max(jnp.abs(delta), axis=1, keepdims=True)
                scale = (top + tiny_eps).astype(jnp.bfloat16).astype(jnp.float32)
                levels = (delta * (1.0 / scale)).astype(jnp.bfloat16)
                total = total + levels.astype(jnp.float32) * scale
            average = total * (1.0 / groups)
            new_moment = outer_mu * moment_ref[at, cols] + average
            new_moment_ref[at, cols] = new_moment
            new_outer_ref[at, cols] = (
                outer - outer_rate * (average + outer_mu * new_moment)
            ).astype(new_outer_ref.dtype)
        return carry

    lax.fori_loop(0, rows // strip, step, 0)


def outer_update(first, steps, tile, me, outer, moment, weight, pieces, previous, *after):
    width = outer.shape[1]
    strip = 32 if tile % 32 == 0 else 16
    groups = len(pieces) + 1
    placed = pl.BlockSpec((tile, width), lambda i, me: (first + i, 0))
    in_specs = [
        placed,
        placed,
        pl.BlockSpec((1, tile, width), lambda i, me: (0, first + i, me[0])),
    ] + [
        pl.BlockSpec((tile, width), lambda i, me, skip=first - begin: (skip + i, 0))
        for _, begin in pieces
    ]
    args = [me, outer, moment, weight] + [piece for piece, _ in pieces]
    aliases = {}
    if previous is not None:
        aliases = {len(args): 0, len(args) + 1: 1}
        in_specs += [STAY] * 2
        args += list(previous)
    in_specs += [STAY] * len(after)
    args += list(after)
    *updated, token = pl.pallas_call(
        functools.partial(outer_kernel, groups, strip),
        grid_spec=pltpu.PrefetchScalarGridSpec(
            num_scalar_prefetch=1,
            grid=(steps,),
            in_specs=in_specs,
            out_specs=[placed, placed, TOKEN_SPEC],
        ),
        out_shape=[
            jax.ShapeDtypeStruct(outer.shape, outer.dtype),
            jax.ShapeDtypeStruct(moment.shape, moment.dtype),
            TOKEN,
        ],
        input_output_aliases=aliases,
        cost_estimate=BRIEF,
        compiler_params=pltpu.CompilerParams(vmem_limit_bytes=VMEM_LIMIT),
        name="outer_update",
    )(*args)
    return updated, token


def per_device(tokens, readout, resp_mask, order, w_gate, w_up, outer_gate, outer_up, moment):
    groups = lax.axis_size("rep")
    ranks = lax.axis_size("fsdp")
    place = lax.axis_index("rep").reshape(1).astype(jnp.int32)
    width = outer_gate.shape[1]

    def swap(value, bits):
        return lax.ppermute(value, "rep", [(i, i ^ bits) for i in range(groups)])

    tile = outer_gate.shape[0] // sum(CHUNKS)
    starts = [sum(CHUNKS[:chunk]) for chunk in range(len(CHUNKS))]
    pieces = [[] for _ in CHUNKS]
    updated = None

    def send(chunks, masks, *after):
        steps = sum(CHUNKS[chunk] for chunk in chunks)
        begin = starts[chunks[0]]
        parts, token = pick(begin, steps, tile, place, w_gate, masks, width, *after)
        came = [swap(part, bits) for part, bits in zip(parts, masks)]
        for chunk in chunks:
            pieces[chunk] += [(piece, begin) for piece in came]
        return came, token

    def update(chunk, *after):
        return outer_update(
            starts[chunk],
            CHUNKS[chunk],
            tile,
            place,
            outer_gate,
            moment,
            w_gate,
            pieces[chunk],
            updated,
            *after,
        )

    first, token = send((0,), (2,))
    shares, token = pick(
        0, 1, tokens.shape[0], place, tokens[None], tuple(range(1, groups)), width, token
    )
    others = [swap(share, bits) for bits, share in enumerate(shares, 1)]
    assembled, token = assemble(place, tokens, others, token)
    gathered = lax.all_gather(assembled, "fsdp", axis=0, tiled=False)
    _, token = send((0,), (1, 3), token)
    second, token = send((1,), (2,), token, *first)
    updated, token = update(0, token)

    *parts, token = partial_products(gathered, outer_gate, outer_up, token)
    for at in (1, 3, 5, 7):
        parts[at] = swap(parts[at], 1)
    leave_gate, leave_up, stay_gate, stay_up, token = join(parts)
    gate_ref = stay_gate + swap(leave_gate, 2).astype(jnp.float32)
    upper_ref = stay_up + swap(leave_up, 2).astype(jnp.float32)
    _, token = send((1,), (1, 3), token)
    third, token = send((2,), (2,), token, *second)
    gate, upper, inputs, token = policy_products(gathered, w_gate, w_up, token)

    group_tok = inputs.shape[0]
    seqs = group_tok // LEN
    mask_f = resp_mask.astype(jnp.float32)
    hidden = (jax.nn.silu(gate) * upper).astype(jnp.bfloat16)
    hidden_ref = (jax.nn.silu(gate_ref) * upper_ref).astype(jnp.bfloat16)
    relative = local_scores(hidden, readout, mask_f, seqs) - local_scores(
        hidden_ref, readout, mask_f, seqs
    )
    hop = 1
    while hop < ranks:
        relative = relative + lax.ppermute(
            relative, "fsdp", [(i, i ^ hop) for i in range(ranks)]
        )
        hop *= 2
    places = jnp.arange(seqs, dtype=jnp.int32)
    pick_chosen = (order[0, 0::2][:, None] == places[None, :]).astype(jnp.float32)
    pick_rejected = (order[0, 1::2][:, None] == places[None, :]).astype(jnp.float32)
    highest = lax.Precision.HIGHEST
    margin = dpo_beta * (
        jnp.dot(pick_chosen, relative, precision=highest)
        - jnp.dot(pick_rejected, relative, precision=highest)
    )
    loss = jnp.mean(jax.nn.softplus(-margin)).reshape(1)
    weight = dpo_beta * jax.nn.sigmoid(-margin) / pick_chosen.shape[0]
    coef = jnp.dot(weight, pick_rejected - pick_chosen, precision=highest)
    token_grad = jnp.broadcast_to(coef[:, None], (seqs, LEN)).reshape(-1) * mask_f
    grad_gate, grad_up, token = weight_grads(gate, upper, readout, token_grad, inputs, token)
    _, token = send((2,), (1, 3), token)
    updated, token = update(1, token)
    _, token = send((3,), (1, 2, 3), token)
    updated, token = update(2, token)
    _, token = send((4,), (1, 2, 3), token)
    updated, token = update(3, token)
    updated, token = update(4, token)
    new_outer, new_moment = updated
    return (loss, grad_gate, grad_up, new_outer, new_moment)


def solution(mesh):
    return jax.shard_map(
        per_device,
        mesh=mesh,
        in_specs=(
            P(("rep", "fsdp"), None),
            P("rep", "fsdp"),
            P("rep"),
            P("rep", None),
            P("rep", "fsdp", None),
            P("rep", "fsdp", None),
            P("fsdp", "rep"),
            P("fsdp", "rep"),
            P("fsdp", "rep"),
        ),
        out_specs=(
            P("rep"),
            P("rep", "fsdp", None),
            P("rep", "fsdp", None),
            P("fsdp", "rep"),
            P("fsdp", "rep"),
        ),
        check_vma=False,
    )
```

```python
import functools

import jax
import jax.numpy as jnp
from jax import lax
from jax.experimental import pallas as pl
from jax.experimental.pallas import tpu as pltpu
from jax.sharding import PartitionSpec as P

BLOCK = 128
LEN = 16
TILES = 14
VMEM_LIMIT = 60 * 1024 * 1024
BRIEF = pl.CostEstimate(flops=1, bytes_accessed=1, transcendentals=0)

dpo_beta = 0.1
outer_rate = 0.7
outer_mu = 0.9
tiny_eps = 1e-06


def project(rows, weight):
    return lax.dot_general(
        rows, weight, (((1,), (1,)), ((), ())), preferred_element_type=jnp.float32
    )


def local_scores(hidden, readout, mask_f, seqs):
    per_token = jnp.sum(hidden.astype(jnp.float32) * readout.astype(jnp.float32), axis=1)
    return jnp.sum((per_token * mask_f).reshape(seqs, LEN), axis=1)


def tile_of(rows):
    return 256 if rows % 256 == 0 else rows


def mark(token_ref):
    token_ref[...] = jnp.zeros_like(token_ref)


TOKEN = jax.ShapeDtypeStruct((8, 128), jnp.float32)
TOKEN_SPEC = pl.BlockSpec((8, 128), lambda *_: (0, 0))
STAY = pl.BlockSpec(memory_space=pltpu.HBM)


def pick_kernel(count, me_ref, *refs):
    del me_ref
    token_ref = refs[-1]
    mark(token_ref)
    for source_ref, target_ref in zip(refs[:count], refs[-1 - count : -1]):
        target_ref[...] = source_ref[0]


def pick(first, steps, tile, me, weight, masks, width, *after):
    rows = steps * tile
    count = len(masks)
    *parts, token = pl.pallas_call(
        functools.partial(pick_kernel, count),
        grid_spec=pltpu.PrefetchScalarGridSpec(
            num_scalar_prefetch=1,
            grid=(steps,),
            in_specs=[
                pl.BlockSpec(
                    (1, tile, width), lambda i, me, mask=mask: (0, first + i, me[0] ^ mask)
                )
                for mask in masks
            ]
            + [STAY] * len(after),
            out_specs=[pl.BlockSpec((tile, width), lambda i, me: (i, 0))] * count + [TOKEN_SPEC],
        ),
        out_shape=[jax.ShapeDtypeStruct((rows, width), weight.dtype)] * count + [TOKEN],
        cost_estimate=BRIEF,
        compiler_params=pltpu.CompilerParams(vmem_limit_bytes=VMEM_LIMIT),
        name="pick",
    )(me, *[weight] * count, *after)
    return parts, token


def assemble_kernel(groups, me_ref, tokens_ref, *refs):
    out_ref, token_ref = refs[-2:]
    width = out_ref.shape[2]
    mark(token_ref)
    for block in range(groups):
        out_ref[block] = tokens_ref[:, block * width : (block + 1) * width]
    out_ref[groups] = tokens_ref[:, pl.ds(pl.multiple_of(me_ref[0] * width, width), width)]
    for k in range(1, groups):
        out_ref[groups + k] = refs[k - 1][...]


def assemble(me, tokens, others, *after):
    groups = len(others) + 1
    rows, depth = tokens.shape
    width = depth // groups
    whole = pl.BlockSpec((rows, width), lambda i, me: (0, 0))
    return pl.pallas_call(
        functools.partial(assemble_kernel, groups),
        grid_spec=pltpu.PrefetchScalarGridSpec(
            num_scalar_prefetch=1,
            grid=(1,),
            in_specs=[pl.BlockSpec((rows, depth), lambda i, me: (0, 0))] + [whole] * (groups - 1)
            + [STAY] * len(after),
            out_specs=[
                pl.BlockSpec((2 * groups, rows, width), lambda i, me: (0, 0, 0)),
                TOKEN_SPEC,
            ],
        ),
        out_shape=[jax.ShapeDtypeStruct((2 * groups, rows, width), tokens.dtype), TOKEN],
        cost_estimate=BRIEF,
        compiler_params=pltpu.CompilerParams(vmem_limit_bytes=VMEM_LIMIT),
        name="assemble",
    )(me, tokens, *others, *after)


def partial_kernel(shares_ref, gate_ref, up_ref, *refs):
    *results, token_ref = refs[-1 - 2 * shares_ref.shape[1] :]
    ranks, groups, rows, width = shares_ref.shape
    shares = shares_ref[...].reshape(ranks * groups * rows, width)
    mark(token_ref)
    for which, weight_ref in enumerate((gate_ref, up_ref)):
        product = project(shares, weight_ref[...])
        product = product.reshape(ranks, groups, rows, product.shape[1])
        for k in range(groups):
            part = product[:, k].reshape(ranks * rows, product.shape[3])
            target_ref = results[which * groups + k]
            target_ref[...] = part.astype(target_ref.dtype)


def partial_products(gathered, outer_gate, outer_up, *after):
    ranks, doubled, rows, width = gathered.shape
    groups = doubled // 2
    unit_rows = outer_gate.shape[0]
    tile = tile_of(unit_rows)
    group_tok = ranks * rows
    weight = pl.BlockSpec((tile, width), lambda i: (i, 0))
    result = pl.BlockSpec((group_tok, tile), lambda i: (0, i))
    return pl.pallas_call(
        partial_kernel,
        grid=(unit_rows // tile,),
        in_specs=[
            pl.BlockSpec(
                (ranks, groups, rows, width),
                lambda i: (0, 1, 0, 0),
                pipeline_mode=pl.Buffered(1),
            ),
            weight,
            weight,
        ]
        + [STAY] * len(after),
        out_specs=[result] * (2 * groups) + [TOKEN_SPEC],
        out_shape=[
            jax.ShapeDtypeStruct(
                (group_tok, unit_rows), jnp.bfloat16 if k % 2 else jnp.float32
            )
            for _ in range(2)
            for k in range(groups)
        ]
        + [TOKEN],
        compiler_params=pltpu.CompilerParams(vmem_limit_bytes=VMEM_LIMIT),
        cost_estimate=BRIEF,
        name="partial_products",
    )(gathered, outer_gate, outer_up, *after)


def join_kernel(far_gate_ref, both_gate_ref, far_up_ref, both_up_ref, *refs):
    leave_gate_ref, leave_up_ref, token_ref = refs[-3:]
    mark(token_ref)
    for far_ref, both_ref, leave_ref in (
        (far_gate_ref, both_gate_ref, leave_gate_ref),
        (far_up_ref, both_up_ref, leave_up_ref),
    ):
        leave_ref[...] = (far_ref[...] + both_ref[...].astype(jnp.float32)).astype(
            leave_ref.dtype
        )


def join(parts, *after):
    group_tok, unit_rows = parts[0].shape
    tile = unit_rows // 2 if unit_rows % 256 == 0 else unit_rows
    block = pl.BlockSpec((group_tok, tile), lambda i: (0, i))
    leave = jax.ShapeDtypeStruct((group_tok, unit_rows), jnp.bfloat16)
    return pl.pallas_call(
        join_kernel,
        grid=(unit_rows // tile,),
        in_specs=[block] * len(parts) + [STAY] * len(after),
        out_specs=[block] * 2 + [TOKEN_SPEC],
        out_shape=[leave, leave, TOKEN],
        compiler_params=pltpu.CompilerParams(vmem_limit_bytes=VMEM_LIMIT),
        cost_estimate=BRIEF,
        name="join",
    )(*parts, *after)


def policy_kernel(blocks_ref, w_gate_ref, w_up_ref, *refs):
    gate_ref, up_ref, inputs_ref, token_ref, turned_ref = refs[-5:]
    ranks, groups, rows, width = blocks_ref.shape

    @pl.when(pl.program_id(0) == 0)
    def _():
        mark(token_ref)
        for block in range(groups):
            part = blocks_ref[:, block].reshape(ranks * rows, width)
            inputs_ref[:, block * width : (block + 1) * width] = part
            turned_ref[block * width : (block + 1) * width] = part.T

    turned = turned_ref[...]
    for weight_ref, result_ref in ((w_gate_ref, gate_ref), (w_up_ref, up_ref)):
        result_ref[...] = jnp.dot(
            weight_ref[0], turned, preferred_element_type=jnp.float32
        ).T


def policy_products(gathered, w_gate, w_up, *after):
    ranks, doubled, rows, width = gathered.shape
    groups = doubled // 2
    unit_rows, depth = w_gate.shape[1:]
    tile = tile_of(unit_rows)
    group_tok = ranks * rows
    weight = pl.BlockSpec((1, tile, depth), lambda i: (0, i, 0))
    result = pl.BlockSpec((group_tok, tile), lambda i: (0, i))
    return pl.pallas_call(
        policy_kernel,
        grid=(unit_rows // tile,),
        in_specs=[
            pl.BlockSpec(
                (ranks, groups, rows, width),
                lambda i: (0, 0, 0, 0),
                pipeline_mode=pl.Buffered(1),
            ),
            weight,
            weight,
        ]
        + [STAY] * len(after),
        out_specs=[result, result, pl.BlockSpec((group_tok, depth), lambda i: (0, 0)), TOKEN_SPEC],
        out_shape=[
            jax.ShapeDtypeStruct((group_tok, unit_rows), jnp.float32),
            jax.ShapeDtypeStruct((group_tok, unit_rows), jnp.float32),
            jax.ShapeDtypeStruct((group_tok, depth), gathered.dtype),
            TOKEN,
        ],
        scratch_shapes=[pltpu.VMEM((depth, group_tok), gathered.dtype)],
        compiler_params=pltpu.CompilerParams(vmem_limit_bytes=VMEM_LIMIT),
        cost_estimate=BRIEF,
        name="policy_products",
    )(gathered, w_gate, w_up, *after)


def grads_kernel(gate_ref, up_ref, readout_ref, token_grad_ref, inputs_ref, *refs):
    grad_gate_ref, grad_up_ref, token_ref = refs[-3:]
    mark(token_ref)
    gate = gate_ref[...]
    hidden_grad = token_grad_ref[...] * readout_ref[...].astype(jnp.float32)
    sigma = jax.nn.sigmoid(gate)
    gate_grad = hidden_grad * up_ref[...] * sigma * (1.0 + gate * (1.0 - sigma))
    up_grad = hidden_grad * (gate * sigma)
    contract = (((0,), (0,)), ((), ()))
    for target_ref, grad in ((grad_gate_ref, gate_grad), (grad_up_ref, up_grad)):
        target_ref[0] = lax.dot_general(
            grad.astype(jnp.bfloat16),
            inputs_ref[...],
            contract,
            preferred_element_type=jnp.float32,
        ).astype(target_ref.dtype)


def weight_grads(gate, upper, readout, token_grad, inputs, *after):
    group_tok, unit_rows = gate.shape
    depth = inputs.shape[1]
    tile = tile_of(unit_rows)
    units = pl.BlockSpec((group_tok, tile), lambda i: (0, i))
    result = pl.BlockSpec((1, tile, depth), lambda i: (0, i, 0))
    shape = jax.ShapeDtypeStruct((1, unit_rows, depth), jnp.bfloat16)
    return pl.pallas_call(
        grads_kernel,
        grid=(unit_rows // tile,),
        in_specs=[
            units,
            units,
            units,
            pl.BlockSpec((group_tok, 1), lambda i: (0, 0)),
            pl.BlockSpec(
                (group_tok, depth), lambda i: (0, 0), pipeline_mode=pl.Buffered(1)
            ),
        ]
        + [STAY] * len(after),
        out_specs=[result, result, TOKEN_SPEC],
        out_shape=[shape, shape, TOKEN],
        compiler_params=pltpu.CompilerParams(vmem_limit_bytes=VMEM_LIMIT),
        cost_estimate=BRIEF,
        name="weight_grads",
    )(gate, upper, readout, token_grad[:, None], inputs, *after)


def outer_kernel(groups, strip, me_ref, outer_ref, moment_ref, *refs):
    del me_ref
    inner = (refs[0].at[0], *refs[1:groups])
    new_outer_ref, new_moment_ref, token_ref = refs[-3:]
    rows, width = outer_ref.shape
    mark(token_ref)

    def step(index, carry):
        at = pl.ds(pl.multiple_of(index * strip, strip), strip)
        for block in range(width // BLOCK):
            cols = pl.ds(block * BLOCK, BLOCK)
            outer = outer_ref[at, cols].astype(jnp.float32)
            total = jnp.zeros_like(outer)
            for ref in inner:
                delta = outer - ref[at, cols].astype(jnp.float32)
                top = jnp.max(jnp.abs(delta), axis=1, keepdims=True)
                scale = (top + tiny_eps).astype(jnp.bfloat16).astype(jnp.float32)
                levels = (delta * (1.0 / scale)).astype(jnp.bfloat16)
                total = total + levels.astype(jnp.float32) * scale
            average = total * (1.0 / groups)
            new_moment = outer_mu * moment_ref[at, cols] + average
            new_moment_ref[at, cols] = new_moment
            new_outer_ref[at, cols] = (
                outer - outer_rate * (average + outer_mu * new_moment)
            ).astype(new_outer_ref.dtype)
        return carry

    lax.fori_loop(0, rows // strip, step, 0)


def outer_update(first, steps, tile, me, outer, moment, weight, pieces, previous, *after):
    width = outer.shape[1]
    strip = 32 if tile % 32 == 0 else 16
    groups = len(pieces) + 1
    placed = pl.BlockSpec((tile, width), lambda i, me: (first + i, 0))
    in_specs = [
        placed,
        placed,
        pl.BlockSpec((1, tile, width), lambda i, me: (0, first + i, me[0])),
    ] + [
        pl.BlockSpec((tile, width), lambda i, me, skip=first - begin: (skip + i, 0))
        for _, begin in pieces
    ]
    args = [me, outer, moment, weight] + [piece for piece, _ in pieces]
    aliases = {}
    if previous is not None:
        aliases = {len(args): 0, len(args) + 1: 1}
        in_specs += [STAY] * 2
        args += list(previous)
    in_specs += [STAY] * len(after)
    args += list(after)
    *updated, token = pl.pallas_call(
        functools.partial(outer_kernel, groups, strip),
        grid_spec=pltpu.PrefetchScalarGridSpec(
            num_scalar_prefetch=1,
            grid=(steps,),
            in_specs=in_specs,
            out_specs=[placed, placed, TOKEN_SPEC],
        ),
        out_shape=[
            jax.ShapeDtypeStruct(outer.shape, outer.dtype),
            jax.ShapeDtypeStruct(moment.shape, moment.dtype),
            TOKEN,
        ],
        input_output_aliases=aliases,
        cost_estimate=BRIEF,
        compiler_params=pltpu.CompilerParams(vmem_limit_bytes=VMEM_LIMIT),
        name="outer_update",
    )(*args)
    return updated, token


def per_device(tokens, readout, resp_mask, order, w_gate, w_up, outer_gate, outer_up, moment):
    groups = lax.axis_size("rep")
    ranks = lax.axis_size("fsdp")
    place = lax.axis_index("rep").reshape(1).astype(jnp.int32)
    width = outer_gate.shape[1]

    def swap(value, bits):
        return lax.ppermute(value, "rep", [(i, i ^ bits) for i in range(groups)])

    tile = outer_gate.shape[0] // TILES
    pieces = []
    updated = None

    def send(begin, steps, masks, *after):
        parts, token = pick(begin, steps, tile, place, w_gate, masks, width, *after)
        came = [swap(part, mask) for part, mask in zip(parts, masks)]
        pieces.extend((mask, begin, steps, piece) for mask, piece in zip(masks, came))
        return came, token

    def update(first, steps, *after):
        there = [
            (piece, begin)
            for mask, begin, count, piece in pieces
            if begin <= first and first + steps <= begin + count
        ]
        assert len(there) == groups - 1
        return outer_update(
            first, steps, tile, place, outer_gate, moment, w_gate, there, updated, *after
        )

    early, token = send(0, 6, (2,))
    shares, token = pick(
        0, 1, tokens.shape[0], place, tokens[None], tuple(range(1, groups)), width, token
    )
    others = [swap(share, bits) for bits, share in enumerate(shares, 1)]
    assembled, token = assemble(place, tokens, others, token)
    gathered = lax.all_gather(assembled, "fsdp", axis=0, tiled=False)
    _, token = send(0, 3, (1, 3), token)
    late, token = send(3, 3, (1, 3), token, *early)
    updated, token = update(0, 3, token)
    second, token = send(6, 4, (2,), token)

    *parts, token = partial_products(gathered, outer_gate, outer_up, token, *late)
    for at in (1, 3, 5, 7):
        parts[at] = swap(parts[at], 1)
    stay_gate, near_gate, far_gate, both_gate, stay_up, near_up, far_up, both_up = parts
    leave_gate, leave_up, token = join(
        (far_gate, both_gate, far_up, both_up), near_gate, near_up
    )
    gate_ref, upper_ref = (
        stay + near.astype(jnp.float32) + swap(leave, 2).astype(jnp.float32)
        for stay, near, leave in (
            (stay_gate, near_gate, leave_gate),
            (stay_up, near_up, leave_up),
        )
    )
    _, token = send(6, 4, (1, 3), token)
    _, token = send(10, 2, (2,), token, *second)
    gate, upper, inputs, token = policy_products(gathered, w_gate, w_up, token)
    _, token = send(10, 2, (1, 3), token)
    updated, token = update(3, 3, token)

    group_tok = inputs.shape[0]
    seqs = group_tok // LEN
    mask_f = resp_mask.astype(jnp.float32)
    hidden = (jax.nn.silu(gate) * upper).astype(jnp.bfloat16)
    hidden_ref = (jax.nn.silu(gate_ref) * upper_ref).astype(jnp.bfloat16)
    relative = local_scores(hidden, readout, mask_f, seqs) - local_scores(
        hidden_ref, readout, mask_f, seqs
    )
    hop = 1
    while hop < ranks:
        relative = relative + lax.ppermute(
            relative, "fsdp", [(i, i ^ hop) for i in range(ranks)]
        )
        hop *= 2
    places = jnp.arange(seqs, dtype=jnp.int32)
    pick_chosen = (order[0, 0::2][:, None] == places[None, :]).astype(jnp.float32)
    pick_rejected = (order[0, 1::2][:, None] == places[None, :]).astype(jnp.float32)
    highest = lax.Precision.HIGHEST
    margin = dpo_beta * (
        jnp.dot(pick_chosen, relative, precision=highest)
        - jnp.dot(pick_rejected, relative, precision=highest)
    )
    loss = jnp.mean(jax.nn.softplus(-margin)).reshape(1)
    weight = dpo_beta * jax.nn.sigmoid(-margin) / pick_chosen.shape[0]
    coef = jnp.dot(weight, pick_rejected - pick_chosen, precision=highest)
    token_grad = jnp.broadcast_to(coef[:, None], (seqs, LEN)).reshape(-1) * mask_f
    grad_gate, grad_up, token = weight_grads(gate, upper, readout, token_grad, inputs, token)
    _, token = send(12, 1, (1, 2, 3), token)
    updated, token = update(6, 4, token)
    _, token = send(13, 1, (1, 2, 3), token)
    updated, token = update(10, 2, token)
    updated, token = update(12, 1, token)
    updated, token = update(13, 1, token)
    new_outer, new_moment = updated
    return (loss, grad_gate, grad_up, new_outer, new_moment)


def solution(mesh):
    return jax.shard_map(
        per_device,
        mesh=mesh,
        in_specs=(
            P(("rep", "fsdp"), None),
            P("rep", "fsdp"),
            P("rep"),
            P("rep", None),
            P("rep", "fsdp", None),
            P("rep", "fsdp", None),
            P("fsdp", "rep"),
            P("fsdp", "rep"),
            P("fsdp", "rep"),
        ),
        out_specs=(
            P("rep"),
            P("rep", "fsdp", None),
            P("rep", "fsdp", None),
            P("fsdp", "rep"),
            P("fsdp", "rep"),
        ),
        check_vma=False,
    )
```

```python
import functools

import jax
import jax.numpy as jnp
from jax import lax
from jax.experimental import pallas as pl
from jax.experimental.pallas import tpu as pltpu
from jax.sharding import PartitionSpec as P

BLOCK = 128
LEN = 16
TILES = 14
VMEM_LIMIT = 60 * 1024 * 1024
BRIEF = pl.CostEstimate(flops=1, bytes_accessed=1, transcendentals=0)

dpo_beta = 0.1
outer_rate = 0.7
outer_mu = 0.9
tiny_eps = 1e-06


def project(rows, weight):
    return lax.dot_general(
        rows, weight, (((1,), (1,)), ((), ())), preferred_element_type=jnp.float32
    )


def local_scores(hidden, readout, mask_f, seqs):
    per_token = jnp.sum(hidden.astype(jnp.float32) * readout.astype(jnp.float32), axis=1)
    return jnp.sum((per_token * mask_f).reshape(seqs, LEN), axis=1)


def tile_of(rows):
    return 256 if rows % 256 == 0 else rows


def mark(token_ref):
    token_ref[...] = jnp.zeros_like(token_ref)


TOKEN = jax.ShapeDtypeStruct((8, 128), jnp.float32)
TOKEN_SPEC = pl.BlockSpec((8, 128), lambda *_: (0, 0))
STAY = pl.BlockSpec(memory_space=pltpu.HBM)


def pick_kernel(count, me_ref, *refs):
    del me_ref
    token_ref = refs[-1]
    mark(token_ref)
    for source_ref, target_ref in zip(refs[:count], refs[-1 - count : -1]):
        target_ref[...] = source_ref[0]


def pick(first, steps, tile, me, weight, masks, width, *after):
    rows = steps * tile
    block = max(
        size
        for size in range(1, max(1, steps // 2) + 1)
        if steps % size == 0 and first % size == 0
    )
    first, steps, tile = first // block, steps // block, tile * block
    count = len(masks)
    *parts, token = pl.pallas_call(
        functools.partial(pick_kernel, count),
        grid_spec=pltpu.PrefetchScalarGridSpec(
            num_scalar_prefetch=1,
            grid=(steps,),
            in_specs=[
                pl.BlockSpec(
                    (1, tile, width), lambda i, me, mask=mask: (0, first + i, me[0] ^ mask)
                )
                for mask in masks
            ]
            + [STAY] * len(after),
            out_specs=[pl.BlockSpec((tile, width), lambda i, me: (i, 0))] * count + [TOKEN_SPEC],
        ),
        out_shape=[jax.ShapeDtypeStruct((rows, width), weight.dtype)] * count + [TOKEN],
        cost_estimate=BRIEF,
        compiler_params=pltpu.CompilerParams(vmem_limit_bytes=VMEM_LIMIT),
        name="pick",
    )(me, *[weight] * count, *after)
    return parts, token


def assemble_kernel(groups, me_ref, tokens_ref, *refs):
    out_ref, token_ref = refs[-2:]
    width = out_ref.shape[2]
    mark(token_ref)
    for block in range(groups):
        out_ref[block] = tokens_ref[:, block * width : (block + 1) * width]
    out_ref[groups] = tokens_ref[:, pl.ds(pl.multiple_of(me_ref[0] * width, width), width)]
    for k in range(1, groups):
        out_ref[groups + k] = refs[k - 1][...]


def assemble(me, tokens, others, *after):
    groups = len(others) + 1
    rows, depth = tokens.shape
    width = depth // groups
    whole = pl.BlockSpec((rows, width), lambda i, me: (0, 0))
    return pl.pallas_call(
        functools.partial(assemble_kernel, groups),
        grid_spec=pltpu.PrefetchScalarGridSpec(
            num_scalar_prefetch=1,
            grid=(1,),
            in_specs=[pl.BlockSpec((rows, depth), lambda i, me: (0, 0))] + [whole] * (groups - 1)
            + [STAY] * len(after),
            out_specs=[
                pl.BlockSpec((2 * groups, rows, width), lambda i, me: (0, 0, 0)),
                TOKEN_SPEC,
            ],
        ),
        out_shape=[jax.ShapeDtypeStruct((2 * groups, rows, width), tokens.dtype), TOKEN],
        cost_estimate=BRIEF,
        compiler_params=pltpu.CompilerParams(vmem_limit_bytes=VMEM_LIMIT),
        name="assemble",
    )(me, tokens, *others, *after)


def partial_kernel(shares_ref, gate_ref, up_ref, *refs):
    *results, token_ref = refs[-1 - 2 * shares_ref.shape[1] :]
    ranks, groups, rows, width = shares_ref.shape
    shares = shares_ref[...].reshape(ranks * groups * rows, width)
    mark(token_ref)
    for which, weight_ref in enumerate((gate_ref, up_ref)):
        product = project(shares, weight_ref[...])
        product = product.reshape(ranks, groups, rows, product.shape[1])
        for k in range(groups):
            part = product[:, k].reshape(ranks * rows, product.shape[3])
            target_ref = results[which * groups + k]
            target_ref[...] = part.astype(target_ref.dtype)


def partial_products(gathered, outer_gate, outer_up, *after):
    ranks, doubled, rows, width = gathered.shape
    groups = doubled // 2
    unit_rows = outer_gate.shape[0]
    tile = tile_of(unit_rows)
    group_tok = ranks * rows
    weight = pl.BlockSpec((tile, width), lambda i: (i, 0))
    result = pl.BlockSpec((group_tok, tile), lambda i: (0, i))
    return pl.pallas_call(
        partial_kernel,
        grid=(unit_rows // tile,),
        in_specs=[
            pl.BlockSpec(
                (ranks, groups, rows, width),
                lambda i: (0, 1, 0, 0),
                pipeline_mode=pl.Buffered(1),
            ),
            weight,
            weight,
        ]
        + [STAY] * len(after),
        out_specs=[result] * (2 * groups) + [TOKEN_SPEC],
        out_shape=[
            jax.ShapeDtypeStruct(
                (group_tok, unit_rows), jnp.bfloat16 if k % 2 else jnp.float32
            )
            for _ in range(2)
            for k in range(groups)
        ]
        + [TOKEN],
        compiler_params=pltpu.CompilerParams(vmem_limit_bytes=VMEM_LIMIT),
        cost_estimate=BRIEF,
        name="partial_products",
    )(gathered, outer_gate, outer_up, *after)


def join_kernel(far_gate_ref, both_gate_ref, far_up_ref, both_up_ref, *refs):
    leave_gate_ref, leave_up_ref, token_ref = refs[-3:]
    mark(token_ref)
    for far_ref, both_ref, leave_ref in (
        (far_gate_ref, both_gate_ref, leave_gate_ref),
        (far_up_ref, both_up_ref, leave_up_ref),
    ):
        leave_ref[...] = (far_ref[...] + both_ref[...].astype(jnp.float32)).astype(
            leave_ref.dtype
        )


def join(parts, *after):
    group_tok, unit_rows = parts[0].shape
    tile = unit_rows // 2 if unit_rows % 256 == 0 else unit_rows
    block = pl.BlockSpec((group_tok, tile), lambda i: (0, i))
    leave = jax.ShapeDtypeStruct((group_tok, unit_rows), jnp.bfloat16)
    return pl.pallas_call(
        join_kernel,
        grid=(unit_rows // tile,),
        in_specs=[block] * len(parts) + [STAY] * len(after),
        out_specs=[block] * 2 + [TOKEN_SPEC],
        out_shape=[leave, leave, TOKEN],
        compiler_params=pltpu.CompilerParams(vmem_limit_bytes=VMEM_LIMIT),
        cost_estimate=BRIEF,
        name="join",
    )(*parts, *after)


def policy_kernel(blocks_ref, w_gate_ref, w_up_ref, *refs):
    gate_ref, up_ref, inputs_ref, token_ref, turned_ref = refs[-5:]
    ranks, groups, rows, width = blocks_ref.shape

    @pl.when(pl.program_id(0) == 0)
    def _():
        mark(token_ref)
        for block in range(groups):
            part = blocks_ref[:, block].reshape(ranks * rows, width)
            inputs_ref[:, block * width : (block + 1) * width] = part
            turned_ref[block * width : (block + 1) * width] = part.T

    turned = turned_ref[...]
    for weight_ref, result_ref in ((w_gate_ref, gate_ref), (w_up_ref, up_ref)):
        result_ref[...] = jnp.dot(
            weight_ref[0], turned, preferred_element_type=jnp.float32
        ).T


def policy_products(gathered, w_gate, w_up, *after):
    ranks, doubled, rows, width = gathered.shape
    groups = doubled // 2
    unit_rows, depth = w_gate.shape[1:]
    tile = tile_of(unit_rows)
    group_tok = ranks * rows
    weight = pl.BlockSpec((1, tile, depth), lambda i: (0, i, 0))
    result = pl.BlockSpec((group_tok, tile), lambda i: (0, i))
    return pl.pallas_call(
        policy_kernel,
        grid=(unit_rows // tile,),
        in_specs=[
            pl.BlockSpec(
                (ranks, groups, rows, width),
                lambda i: (0, 0, 0, 0),
                pipeline_mode=pl.Buffered(1),
            ),
            weight,
            weight,
        ]
        + [STAY] * len(after),
        out_specs=[result, result, pl.BlockSpec((group_tok, depth), lambda i: (0, 0)), TOKEN_SPEC],
        out_shape=[
            jax.ShapeDtypeStruct((group_tok, unit_rows), jnp.float32),
            jax.ShapeDtypeStruct((group_tok, unit_rows), jnp.float32),
            jax.ShapeDtypeStruct((group_tok, depth), gathered.dtype),
            TOKEN,
        ],
        scratch_shapes=[pltpu.VMEM((depth, group_tok), gathered.dtype)],
        compiler_params=pltpu.CompilerParams(vmem_limit_bytes=VMEM_LIMIT),
        cost_estimate=BRIEF,
        name="policy_products",
    )(gathered, w_gate, w_up, *after)


def grads_kernel(gate_ref, up_ref, readout_ref, token_grad_ref, inputs_ref, *refs):
    grad_gate_ref, grad_up_ref, token_ref = refs[-3:]
    mark(token_ref)
    gate = gate_ref[...]
    hidden_grad = token_grad_ref[...] * readout_ref[...].astype(jnp.float32)
    sigma = jax.nn.sigmoid(gate)
    gate_grad = hidden_grad * up_ref[...] * sigma * (1.0 + gate * (1.0 - sigma))
    up_grad = hidden_grad * (gate * sigma)
    contract = (((0,), (0,)), ((), ()))
    for target_ref, grad in ((grad_gate_ref, gate_grad), (grad_up_ref, up_grad)):
        target_ref[0] = lax.dot_general(
            grad.astype(jnp.bfloat16),
            inputs_ref[...],
            contract,
            preferred_element_type=jnp.float32,
        ).astype(target_ref.dtype)


def weight_grads(gate, upper, readout, token_grad, inputs, *after):
    group_tok, unit_rows = gate.shape
    depth = inputs.shape[1]
    tile = tile_of(unit_rows)
    units = pl.BlockSpec((group_tok, tile), lambda i: (0, i))
    result = pl.BlockSpec((1, tile, depth), lambda i: (0, i, 0))
    shape = jax.ShapeDtypeStruct((1, unit_rows, depth), jnp.bfloat16)
    return pl.pallas_call(
        grads_kernel,
        grid=(unit_rows // tile,),
        in_specs=[
            units,
            units,
            units,
            pl.BlockSpec((group_tok, 1), lambda i: (0, 0)),
            pl.BlockSpec(
                (group_tok, depth), lambda i: (0, 0), pipeline_mode=pl.Buffered(1)
            ),
        ]
        + [STAY] * len(after),
        out_specs=[result, result, TOKEN_SPEC],
        out_shape=[shape, shape, TOKEN],
        compiler_params=pltpu.CompilerParams(vmem_limit_bytes=VMEM_LIMIT),
        cost_estimate=BRIEF,
        name="weight_grads",
    )(gate, upper, readout, token_grad[:, None], inputs, *after)


def outer_kernel(groups, strip, me_ref, outer_ref, moment_ref, *refs):
    del me_ref
    inner = (refs[0].at[0], *refs[1:groups])
    new_outer_ref, new_moment_ref, token_ref = refs[-3:]
    rows, width = outer_ref.shape
    mark(token_ref)

    def step(index, carry):
        at = pl.ds(pl.multiple_of(index * strip, strip), strip)
        for block in range(width // BLOCK):
            cols = pl.ds(block * BLOCK, BLOCK)
            outer = outer_ref[at, cols].astype(jnp.float32)
            total = jnp.zeros_like(outer)
            for ref in inner:
                delta = outer - ref[at, cols].astype(jnp.float32)
                top = jnp.max(jnp.abs(delta), axis=1, keepdims=True)
                scale = (top + tiny_eps).astype(jnp.bfloat16).astype(jnp.float32)
                levels = (delta * (1.0 / scale)).astype(jnp.bfloat16)
                total = total + levels.astype(jnp.float32) * scale
            average = total * (1.0 / groups)
            new_moment = outer_mu * moment_ref[at, cols] + average
            new_moment_ref[at, cols] = new_moment
            new_outer_ref[at, cols] = (
                outer - outer_rate * (average + outer_mu * new_moment)
            ).astype(new_outer_ref.dtype)
        return carry

    lax.fori_loop(0, rows // strip, step, 0)


def outer_update(first, steps, tile, me, outer, moment, weight, pieces, previous, *after):
    width = outer.shape[1]
    strip = 32 if tile % 32 == 0 else 16
    groups = len(pieces) + 1
    placed = pl.BlockSpec((tile, width), lambda i, me: (first + i, 0))
    in_specs = [
        placed,
        placed,
        pl.BlockSpec((1, tile, width), lambda i, me: (0, first + i, me[0])),
    ] + [
        pl.BlockSpec((tile, width), lambda i, me, skip=first - begin: (skip + i, 0))
        for _, begin in pieces
    ]
    args = [me, outer, moment, weight] + [piece for piece, _ in pieces]
    aliases = {}
    if previous is not None:
        aliases = {len(args): 0, len(args) + 1: 1}
        in_specs += [STAY] * 2
        args += list(previous)
    in_specs += [STAY] * len(after)
    args += list(after)
    *updated, token = pl.pallas_call(
        functools.partial(outer_kernel, groups, strip),
        grid_spec=pltpu.PrefetchScalarGridSpec(
            num_scalar_prefetch=1,
            grid=(steps,),
            in_specs=in_specs,
            out_specs=[placed, placed, TOKEN_SPEC],
        ),
        out_shape=[
            jax.ShapeDtypeStruct(outer.shape, outer.dtype),
            jax.ShapeDtypeStruct(moment.shape, moment.dtype),
            TOKEN,
        ],
        input_output_aliases=aliases,
        cost_estimate=BRIEF,
        compiler_params=pltpu.CompilerParams(vmem_limit_bytes=VMEM_LIMIT),
        name="outer_update",
    )(*args)
    return updated, token


def per_device(tokens, readout, resp_mask, order, w_gate, w_up, outer_gate, outer_up, moment):
    groups = lax.axis_size("rep")
    ranks = lax.axis_size("fsdp")
    place = lax.axis_index("rep").reshape(1).astype(jnp.int32)
    width = outer_gate.shape[1]

    def swap(value, bits):
        return lax.ppermute(value, "rep", [(i, i ^ bits) for i in range(groups)])

    tile = outer_gate.shape[0] // TILES
    pieces = []
    updated = None

    def send(begin, steps, masks, *after):
        parts, token = pick(begin, steps, tile, place, w_gate, masks, width, *after)
        came = [swap(part, mask) for part, mask in zip(parts, masks)]
        pieces.extend((mask, begin, steps, piece) for mask, piece in zip(masks, came))
        return came, token

    def update(first, steps, *after):
        there = [
            (piece, begin)
            for mask, begin, count, piece in pieces
            if begin <= first and first + steps <= begin + count
        ]
        assert len(there) == groups - 1
        return outer_update(
            first, steps, tile, place, outer_gate, moment, w_gate, there, updated, *after
        )

    early, token = send(0, 10, (2,))
    shares, token = pick(
        0, 1, tokens.shape[0], place, tokens[None], tuple(range(1, groups)), width, token
    )
    others = [swap(share, bits) for bits, share in enumerate(shares, 1)]
    assembled, token = assemble(place, tokens, others, token)
    gathered = lax.all_gather(assembled, "fsdp", axis=0, tiled=False)
    (near, _), token = send(0, 6, (1, 3), token)

    *parts, token = partial_products(gathered, outer_gate, outer_up, token, near, *early)
    for at in (1, 3, 5, 7):
        parts[at] = swap(parts[at], 1)
    stay_gate, near_gate, far_gate, both_gate, stay_up, near_up, far_up, both_up = parts
    leave_gate, leave_up, token = join(
        (far_gate, both_gate, far_up, both_up), near_gate, near_up
    )
    gate_ref, upper_ref = (
        stay + near.astype(jnp.float32) + swap(leave, 2).astype(jnp.float32)
        for stay, near, leave in (
            (stay_gate, near_gate, leave_gate),
            (stay_up, near_up, leave_up),
        )
    )
    _, token = send(6, 4, (1, 3), token)
    gate, upper, inputs, token = policy_products(gathered, w_gate, w_up, token)
    updated, token = update(0, 6, token)

    group_tok = inputs.shape[0]
    seqs = group_tok // LEN
    mask_f = resp_mask.astype(jnp.float32)
    hidden = (jax.nn.silu(gate) * upper).astype(jnp.bfloat16)
    hidden_ref = (jax.nn.silu(gate_ref) * upper_ref).astype(jnp.bfloat16)
    relative = local_scores(hidden, readout, mask_f, seqs) - local_scores(
        hidden_ref, readout, mask_f, seqs
    )
    _, token = send(10, 2, (1, 2, 3), token, relative[None])
    hop = 1
    while hop < ranks:
        relative = relative + lax.ppermute(
            relative, "fsdp", [(i, i ^ hop) for i in range(ranks)]
        )
        hop *= 2
    places = jnp.arange(seqs, dtype=jnp.int32)
    pick_chosen = (order[0, 0::2][:, None] == places[None, :]).astype(jnp.float32)
    pick_rejected = (order[0, 1::2][:, None] == places[None, :]).astype(jnp.float32)
    highest = lax.Precision.HIGHEST
    margin = dpo_beta * (
        jnp.dot(pick_chosen, relative, precision=highest)
        - jnp.dot(pick_rejected, relative, precision=highest)
    )
    loss = jnp.mean(jax.nn.softplus(-margin)).reshape(1)
    weight = dpo_beta * jax.nn.sigmoid(-margin) / pick_chosen.shape[0]
    coef = jnp.dot(weight, pick_rejected - pick_chosen, precision=highest)
    token_grad = jnp.broadcast_to(coef[:, None], (seqs, LEN)).reshape(-1) * mask_f
    grad_gate, grad_up, token = weight_grads(gate, upper, readout, token_grad, inputs, token)
    _, token = send(12, 1, (1, 2, 3), token)
    updated, token = update(6, 4, token)
    _, token = send(13, 1, (1, 2, 3), token)
    updated, token = update(10, 2, token)
    updated, token = update(12, 1, token)
    updated, token = update(13, 1, token)
    new_outer, new_moment = updated
    return (loss, grad_gate, grad_up, new_outer, new_moment)


def solution(mesh):
    return jax.shard_map(
        per_device,
        mesh=mesh,
        in_specs=(
            P(("rep", "fsdp"), None),
            P("rep", "fsdp"),
            P("rep"),
            P("rep", None),
            P("rep", "fsdp", None),
            P("rep", "fsdp", None),
            P("fsdp", "rep"),
            P("fsdp", "rep"),
            P("fsdp", "rep"),
        ),
        out_specs=(
            P("rep"),
            P("rep", "fsdp", None),
            P("rep", "fsdp", None),
            P("fsdp", "rep"),
            P("fsdp", "rep"),
        ),
        check_vma=False,
    )
```

```python
import functools

import jax
import jax.numpy as jnp
from jax import lax
from jax.experimental import pallas as pl
from jax.experimental.pallas import tpu as pltpu
from jax.sharding import PartitionSpec as P

BLOCK = 128
LEN = 16
TILES = 14
VMEM_LIMIT = 60 * 1024 * 1024
BRIEF = pl.CostEstimate(flops=1, bytes_accessed=1, transcendentals=0)

dpo_beta = 0.1
outer_rate = 0.7
outer_mu = 0.9
tiny_eps = 1e-06


def project(rows, weight):
    return lax.dot_general(
        rows, weight, (((1,), (1,)), ((), ())), preferred_element_type=jnp.float32
    )


def local_scores(hidden, readout, mask_f, seqs):
    per_token = jnp.sum(hidden.astype(jnp.float32) * readout.astype(jnp.float32), axis=1)
    return jnp.sum((per_token * mask_f).reshape(seqs, LEN), axis=1)


def tile_of(rows):
    return 256 if rows % 256 == 0 else rows


def mark(token_ref):
    token_ref[...] = jnp.zeros_like(token_ref)


TOKEN = jax.ShapeDtypeStruct((8, 128), jnp.float32)
TOKEN_SPEC = pl.BlockSpec((8, 128), lambda *_: (0, 0))
STAY = pl.BlockSpec(memory_space=pltpu.HBM)


def pick_kernel(count, me_ref, *refs):
    del me_ref
    token_ref = refs[-1]
    mark(token_ref)
    for source_ref, target_ref in zip(refs[:count], refs[-1 - count : -1]):
        target_ref[...] = source_ref[0]


def pick(first, steps, tile, me, weight, masks, width, *after):
    rows = steps * tile
    block = max(
        size
        for size in range(1, max(1, steps // 2) + 1)
        if steps % size == 0 and first % size == 0
    )
    first, steps, tile = first // block, steps // block, tile * block
    count = len(masks)
    *parts, token = pl.pallas_call(
        functools.partial(pick_kernel, count),
        grid_spec=pltpu.PrefetchScalarGridSpec(
            num_scalar_prefetch=1,
            grid=(steps,),
            in_specs=[
                pl.BlockSpec(
                    (1, tile, width), lambda i, me, mask=mask: (0, first + i, me[0] ^ mask)
                )
                for mask in masks
            ]
            + [STAY] * len(after),
            out_specs=[pl.BlockSpec((tile, width), lambda i, me: (i, 0))] * count + [TOKEN_SPEC],
        ),
        out_shape=[jax.ShapeDtypeStruct((rows, width), weight.dtype)] * count + [TOKEN],
        cost_estimate=BRIEF,
        compiler_params=pltpu.CompilerParams(vmem_limit_bytes=VMEM_LIMIT),
        name="pick",
    )(me, *[weight] * count, *after)
    return parts, token


def assemble_kernel(groups, me_ref, tokens_ref, *refs):
    out_ref, token_ref = refs[-2:]
    width = out_ref.shape[2]
    mark(token_ref)
    for block in range(groups):
        out_ref[block] = tokens_ref[:, block * width : (block + 1) * width]
    out_ref[groups] = tokens_ref[:, pl.ds(pl.multiple_of(me_ref[0] * width, width), width)]
    for k in range(1, groups):
        out_ref[groups + k] = refs[k - 1][...]


def assemble(me, tokens, others, *after):
    groups = len(others) + 1
    rows, depth = tokens.shape
    width = depth // groups
    whole = pl.BlockSpec((rows, width), lambda i, me: (0, 0))
    return pl.pallas_call(
        functools.partial(assemble_kernel, groups),
        grid_spec=pltpu.PrefetchScalarGridSpec(
            num_scalar_prefetch=1,
            grid=(1,),
            in_specs=[pl.BlockSpec((rows, depth), lambda i, me: (0, 0))] + [whole] * (groups - 1)
            + [STAY] * len(after),
            out_specs=[
                pl.BlockSpec((2 * groups, rows, width), lambda i, me: (0, 0, 0)),
                TOKEN_SPEC,
            ],
        ),
        out_shape=[jax.ShapeDtypeStruct((2 * groups, rows, width), tokens.dtype), TOKEN],
        cost_estimate=BRIEF,
        compiler_params=pltpu.CompilerParams(vmem_limit_bytes=VMEM_LIMIT),
        name="assemble",
    )(me, tokens, *others, *after)


def partial_kernel(shares_ref, gate_ref, up_ref, *refs):
    *results, token_ref = refs[-1 - 2 * shares_ref.shape[1] :]
    ranks, groups, rows, width = shares_ref.shape
    shares = shares_ref[...].reshape(ranks * groups * rows, width)
    mark(token_ref)
    for which, weight_ref in enumerate((gate_ref, up_ref)):
        product = project(shares, weight_ref[...])
        product = product.reshape(ranks, groups, rows, product.shape[1])
        for k in range(groups):
            part = product[:, k].reshape(ranks * rows, product.shape[3])
            target_ref = results[which * groups + k]
            target_ref[...] = part.astype(target_ref.dtype)


def partial_products(gathered, outer_gate, outer_up, *after):
    ranks, doubled, rows, width = gathered.shape
    groups = doubled // 2
    unit_rows = outer_gate.shape[0]
    tile = tile_of(unit_rows)
    group_tok = ranks * rows
    weight = pl.BlockSpec((tile, width), lambda i: (i, 0))
    result = pl.BlockSpec((group_tok, tile), lambda i: (0, i))
    return pl.pallas_call(
        partial_kernel,
        grid=(unit_rows // tile,),
        in_specs=[
            pl.BlockSpec(
                (ranks, groups, rows, width),
                lambda i: (0, 1, 0, 0),
                pipeline_mode=pl.Buffered(1),
            ),
            weight,
            weight,
        ]
        + [STAY] * len(after),
        out_specs=[result] * (2 * groups) + [TOKEN_SPEC],
        out_shape=[
            jax.ShapeDtypeStruct(
                (group_tok, unit_rows), jnp.bfloat16 if k % 2 else jnp.float32
            )
            for _ in range(2)
            for k in range(groups)
        ]
        + [TOKEN],
        compiler_params=pltpu.CompilerParams(vmem_limit_bytes=VMEM_LIMIT),
        cost_estimate=BRIEF,
        name="partial_products",
    )(gathered, outer_gate, outer_up, *after)


def join_kernel(far_gate_ref, both_gate_ref, far_up_ref, both_up_ref, *refs):
    leave_gate_ref, leave_up_ref, token_ref = refs[-3:]
    mark(token_ref)
    for far_ref, both_ref, leave_ref in (
        (far_gate_ref, both_gate_ref, leave_gate_ref),
        (far_up_ref, both_up_ref, leave_up_ref),
    ):
        leave_ref[...] = (far_ref[...] + both_ref[...].astype(jnp.float32)).astype(
            leave_ref.dtype
        )


def join(parts, *after):
    group_tok, unit_rows = parts[0].shape
    tile = unit_rows // 2 if unit_rows % 256 == 0 else unit_rows
    block = pl.BlockSpec((group_tok, tile), lambda i: (0, i))
    leave = jax.ShapeDtypeStruct((group_tok, unit_rows), jnp.bfloat16)
    return pl.pallas_call(
        join_kernel,
        grid=(unit_rows // tile,),
        in_specs=[block] * len(parts) + [STAY] * len(after),
        out_specs=[block] * 2 + [TOKEN_SPEC],
        out_shape=[leave, leave, TOKEN],
        compiler_params=pltpu.CompilerParams(vmem_limit_bytes=VMEM_LIMIT),
        cost_estimate=BRIEF,
        name="join",
    )(*parts, *after)


def policy_kernel(blocks_ref, w_gate_ref, w_up_ref, *refs):
    gate_ref, up_ref, inputs_ref, token_ref, turned_ref = refs[-5:]
    ranks, groups, rows, width = blocks_ref.shape

    @pl.when(pl.program_id(0) == 0)
    def _():
        mark(token_ref)
        for block in range(groups):
            part = blocks_ref[:, block].reshape(ranks * rows, width)
            inputs_ref[:, block * width : (block + 1) * width] = part
            turned_ref[block * width : (block + 1) * width] = part.T

    turned = turned_ref[...]
    for weight_ref, result_ref in ((w_gate_ref, gate_ref), (w_up_ref, up_ref)):
        result_ref[...] = jnp.dot(
            weight_ref[0], turned, preferred_element_type=jnp.float32
        ).T


def policy_products(gathered, w_gate, w_up, *after):
    ranks, doubled, rows, width = gathered.shape
    groups = doubled // 2
    unit_rows, depth = w_gate.shape[1:]
    tile = tile_of(unit_rows)
    group_tok = ranks * rows
    weight = pl.BlockSpec((1, tile, depth), lambda i: (0, i, 0))
    result = pl.BlockSpec((group_tok, tile), lambda i: (0, i))
    return pl.pallas_call(
        policy_kernel,
        grid=(unit_rows // tile,),
        in_specs=[
            pl.BlockSpec(
                (ranks, groups, rows, width),
                lambda i: (0, 0, 0, 0),
                pipeline_mode=pl.Buffered(1),
            ),
            weight,
            weight,
        ]
        + [STAY] * len(after),
        out_specs=[result, result, pl.BlockSpec((group_tok, depth), lambda i: (0, 0)), TOKEN_SPEC],
        out_shape=[
            jax.ShapeDtypeStruct((group_tok, unit_rows), jnp.float32),
            jax.ShapeDtypeStruct((group_tok, unit_rows), jnp.float32),
            jax.ShapeDtypeStruct((group_tok, depth), gathered.dtype),
            TOKEN,
        ],
        scratch_shapes=[pltpu.VMEM((depth, group_tok), gathered.dtype)],
        compiler_params=pltpu.CompilerParams(vmem_limit_bytes=VMEM_LIMIT),
        cost_estimate=BRIEF,
        name="policy_products",
    )(gathered, w_gate, w_up, *after)


def grads_kernel(gate_ref, up_ref, readout_ref, token_grad_ref, inputs_ref, *refs):
    grad_gate_ref, grad_up_ref, token_ref = refs[-3:]
    mark(token_ref)
    gate = gate_ref[...]
    hidden_grad = token_grad_ref[...] * readout_ref[...].astype(jnp.float32)
    sigma = jax.nn.sigmoid(gate)
    gate_grad = hidden_grad * up_ref[...] * sigma * (1.0 + gate * (1.0 - sigma))
    up_grad = hidden_grad * (gate * sigma)
    contract = (((0,), (0,)), ((), ()))
    for target_ref, grad in ((grad_gate_ref, gate_grad), (grad_up_ref, up_grad)):
        target_ref[0] = lax.dot_general(
            grad.astype(jnp.bfloat16),
            inputs_ref[...],
            contract,
            preferred_element_type=jnp.float32,
        ).astype(target_ref.dtype)


def weight_grads(gate, upper, readout, token_grad, inputs, *after):
    group_tok, unit_rows = gate.shape
    depth = inputs.shape[1]
    tile = tile_of(unit_rows)
    units = pl.BlockSpec((group_tok, tile), lambda i: (0, i))
    result = pl.BlockSpec((1, tile, depth), lambda i: (0, i, 0))
    shape = jax.ShapeDtypeStruct((1, unit_rows, depth), jnp.bfloat16)
    return pl.pallas_call(
        grads_kernel,
        grid=(unit_rows // tile,),
        in_specs=[
            units,
            units,
            units,
            pl.BlockSpec((group_tok, 1), lambda i: (0, 0)),
            pl.BlockSpec(
                (group_tok, depth), lambda i: (0, 0), pipeline_mode=pl.Buffered(1)
            ),
        ]
        + [STAY] * len(after),
        out_specs=[result, result, TOKEN_SPEC],
        out_shape=[shape, shape, TOKEN],
        compiler_params=pltpu.CompilerParams(vmem_limit_bytes=VMEM_LIMIT),
        cost_estimate=BRIEF,
        name="weight_grads",
    )(gate, upper, readout, token_grad[:, None], inputs, *after)


def outer_kernel(groups, strip, me_ref, outer_ref, moment_ref, *refs):
    del me_ref
    inner = (refs[0].at[0], *refs[1:groups])
    new_outer_ref, new_moment_ref, token_ref = refs[-3:]
    rows, width = outer_ref.shape
    mark(token_ref)

    def step(index, carry):
        at = pl.ds(pl.multiple_of(index * strip, strip), strip)
        for block in range(width // BLOCK):
            cols = pl.ds(block * BLOCK, BLOCK)
            outer = outer_ref[at, cols].astype(jnp.float32)
            total = jnp.zeros_like(outer)
            for ref in inner:
                delta = outer - ref[at, cols].astype(jnp.float32)
                top = jnp.max(jnp.abs(delta), axis=1, keepdims=True)
                scale = (top + tiny_eps).astype(jnp.bfloat16).astype(jnp.float32)
                levels = (delta * (1.0 / scale)).astype(jnp.bfloat16)
                total = total + levels.astype(jnp.float32) * scale
            average = total * (1.0 / groups)
            new_moment = outer_mu * moment_ref[at, cols] + average
            new_moment_ref[at, cols] = new_moment
            new_outer_ref[at, cols] = (
                outer - outer_rate * (average + outer_mu * new_moment)
            ).astype(new_outer_ref.dtype)
        return carry

    lax.fori_loop(0, rows // strip, step, 0)


def outer_update(first, steps, tile, me, outer, moment, weight, pieces, previous, *after):
    width = outer.shape[1]
    strip = 32 if tile % 32 == 0 else 16
    groups = len(pieces) + 1
    placed = pl.BlockSpec((tile, width), lambda i, me: (first + i, 0))
    in_specs = [
        placed,
        placed,
        pl.BlockSpec((1, tile, width), lambda i, me: (0, first + i, me[0])),
    ] + [
        pl.BlockSpec((tile, width), lambda i, me, skip=first - begin: (skip + i, 0))
        for _, begin in pieces
    ]
    args = [me, outer, moment, weight] + [piece for piece, _ in pieces]
    aliases = {}
    if previous is not None:
        aliases = {len(args): 0, len(args) + 1: 1}
        in_specs += [STAY] * 2
        args += list(previous)
    in_specs += [STAY] * len(after)
    args += list(after)
    *updated, token = pl.pallas_call(
        functools.partial(outer_kernel, groups, strip),
        grid_spec=pltpu.PrefetchScalarGridSpec(
            num_scalar_prefetch=1,
            grid=(steps,),
            in_specs=in_specs,
            out_specs=[placed, placed, TOKEN_SPEC],
        ),
        out_shape=[
            jax.ShapeDtypeStruct(outer.shape, outer.dtype),
            jax.ShapeDtypeStruct(moment.shape, moment.dtype),
            TOKEN,
        ],
        input_output_aliases=aliases,
        cost_estimate=BRIEF,
        compiler_params=pltpu.CompilerParams(vmem_limit_bytes=VMEM_LIMIT),
        name="outer_update",
    )(*args)
    return updated, token


def per_device(tokens, readout, resp_mask, order, w_gate, w_up, outer_gate, outer_up, moment):
    groups = lax.axis_size("rep")
    ranks = lax.axis_size("fsdp")
    place = lax.axis_index("rep").reshape(1).astype(jnp.int32)
    width = outer_gate.shape[1]

    def swap(value, bits):
        return lax.ppermute(value, "rep", [(i, i ^ bits) for i in range(groups)])

    tile = outer_gate.shape[0] // TILES
    pieces = []
    updated = None

    def send(begin, steps, masks, *after):
        parts, token = pick(begin, steps, tile, place, w_gate, masks, width, *after)
        came = [swap(part, mask) for part, mask in zip(parts, masks)]
        pieces.extend((mask, begin, steps, piece) for mask, piece in zip(masks, came))
        return came, token

    def update(first, steps, *after):
        there = [
            (piece, begin)
            for mask, begin, count, piece in pieces
            if begin <= first and first + steps <= begin + count
        ]
        assert len(there) == groups - 1
        return outer_update(
            first, steps, tile, place, outer_gate, moment, w_gate, there, updated, *after
        )

    first, token = send(0, 2, (2,))
    shares, token = pick(
        0, 1, tokens.shape[0], place, tokens[None], tuple(range(1, groups)), width, token
    )
    others = [swap(share, bits) for bits, share in enumerate(shares, 1)]
    assembled, token = assemble(place, tokens, others, token, *first)
    early, token = send(2, 8, (2,), token)
    gathered = lax.all_gather(assembled, "fsdp", axis=0, tiled=False)
    (near, _), token = send(0, 4, (1, 3), token)

    *parts, token = partial_products(gathered, outer_gate, outer_up, token, near, *early)
    for at in (1, 3, 5, 7):
        parts[at] = swap(parts[at], 1)
    stay_gate, near_gate, far_gate, both_gate, stay_up, near_up, far_up, both_up = parts
    leave_gate, leave_up, token = join(
        (far_gate, both_gate, far_up, both_up), near_gate, near_up
    )
    gate_ref, upper_ref = (
        stay + near.astype(jnp.float32) + swap(leave, 2).astype(jnp.float32)
        for stay, near, leave in (
            (stay_gate, near_gate, leave_gate),
            (stay_up, near_up, leave_up),
        )
    )
    _, token = send(4, 6, (1, 3), token)
    gate, upper, inputs, token = policy_products(gathered, w_gate, w_up, token)
    updated, token = update(0, 2, token)
    updated, token = update(2, 2, token)

    group_tok = inputs.shape[0]
    seqs = group_tok // LEN
    mask_f = resp_mask.astype(jnp.float32)
    hidden = (jax.nn.silu(gate) * upper).astype(jnp.bfloat16)
    hidden_ref = (jax.nn.silu(gate_ref) * upper_ref).astype(jnp.bfloat16)
    relative = local_scores(hidden, readout, mask_f, seqs) - local_scores(
        hidden_ref, readout, mask_f, seqs
    )
    _, token = send(10, 2, (1, 2, 3), token, relative[None])
    hop = 1
    while hop < ranks:
        relative = relative + lax.ppermute(
            relative, "fsdp", [(i, i ^ hop) for i in range(ranks)]
        )
        hop *= 2
    places = jnp.arange(seqs, dtype=jnp.int32)
    pick_chosen = (order[0, 0::2][:, None] == places[None, :]).astype(jnp.float32)
    pick_rejected = (order[0, 1::2][:, None] == places[None, :]).astype(jnp.float32)
    highest = lax.Precision.HIGHEST
    margin = dpo_beta * (
        jnp.dot(pick_chosen, relative, precision=highest)
        - jnp.dot(pick_rejected, relative, precision=highest)
    )
    loss = jnp.mean(jax.nn.softplus(-margin)).reshape(1)
    weight = dpo_beta * jax.nn.sigmoid(-margin) / pick_chosen.shape[0]
    coef = jnp.dot(weight, pick_rejected - pick_chosen, precision=highest)
    token_grad = jnp.broadcast_to(coef[:, None], (seqs, LEN)).reshape(-1) * mask_f
    grad_gate, grad_up, token = weight_grads(gate, upper, readout, token_grad, inputs, token)
    _, token = send(12, 1, (1, 2, 3), token)
    updated, token = update(4, 6, token)
    _, token = send(13, 1, (1, 2, 3), token)
    updated, token = update(10, 2, token)
    updated, token = update(12, 1, token)
    updated, token = update(13, 1, token)
    new_outer, new_moment = updated
    return (loss, grad_gate, grad_up, new_outer, new_moment)


def solution(mesh):
    return jax.shard_map(
        per_device,
        mesh=mesh,
        in_specs=(
            P(("rep", "fsdp"), None),
            P("rep", "fsdp"),
            P("rep"),
            P("rep", None),
            P("rep", "fsdp", None),
            P("rep", "fsdp", None),
            P("fsdp", "rep"),
            P("fsdp", "rep"),
            P("fsdp", "rep"),
        ),
        out_specs=(
            P("rep"),
            P("rep", "fsdp", None),
            P("rep", "fsdp", None),
            P("fsdp", "rep"),
            P("fsdp", "rep"),
        ),
        check_vma=False,
    )
```

```python
import functools

import jax
import jax.numpy as jnp
from jax import lax
from jax.experimental import pallas as pl
from jax.experimental.pallas import tpu as pltpu
from jax.sharding import PartitionSpec as P

BLOCK = 128
LEN = 16
TILES = 14
VMEM_LIMIT = 60 * 1024 * 1024
BRIEF = pl.CostEstimate(flops=1, bytes_accessed=1, transcendentals=0)

dpo_beta = 0.1
outer_rate = 0.7
outer_mu = 0.9
tiny_eps = 1e-06


def project(rows, weight):
    return lax.dot_general(
        rows, weight, (((1,), (1,)), ((), ())), preferred_element_type=jnp.float32
    )


def local_scores(hidden, readout, mask_f, seqs):
    per_token = jnp.sum(hidden.astype(jnp.float32) * readout.astype(jnp.float32), axis=1)
    return jnp.sum((per_token * mask_f).reshape(seqs, LEN), axis=1)


def tile_of(rows):
    return 256 if rows % 256 == 0 else rows


def mark(token_ref):
    token_ref[...] = jnp.zeros_like(token_ref)


TOKEN = jax.ShapeDtypeStruct((8, 128), jnp.float32)
TOKEN_SPEC = pl.BlockSpec((8, 128), lambda *_: (0, 0))
STAY = pl.BlockSpec(memory_space=pltpu.HBM)


def pick_kernel(count, me_ref, *refs):
    del me_ref
    token_ref = refs[-1]
    mark(token_ref)
    for source_ref, target_ref in zip(refs[:count], refs[-1 - count : -1]):
        target_ref[...] = source_ref[0]


def pick(first, steps, tile, me, weight, masks, width, *after):
    rows = steps * tile
    block = max(
        size
        for size in range(1, max(1, steps // 2) + 1)
        if steps % size == 0 and first % size == 0
    )
    first, steps, tile = first // block, steps // block, tile * block
    count = len(masks)
    *parts, token = pl.pallas_call(
        functools.partial(pick_kernel, count),
        grid_spec=pltpu.PrefetchScalarGridSpec(
            num_scalar_prefetch=1,
            grid=(steps,),
            in_specs=[
                pl.BlockSpec(
                    (1, tile, width), lambda i, me, mask=mask: (0, first + i, me[0] ^ mask)
                )
                for mask in masks
            ]
            + [STAY] * len(after),
            out_specs=[pl.BlockSpec((tile, width), lambda i, me: (i, 0))] * count + [TOKEN_SPEC],
        ),
        out_shape=[jax.ShapeDtypeStruct((rows, width), weight.dtype)] * count + [TOKEN],
        cost_estimate=BRIEF,
        compiler_params=pltpu.CompilerParams(vmem_limit_bytes=VMEM_LIMIT),
        name="pick",
    )(me, *[weight] * count, *after)
    return parts, token


def settle_kernel(*refs):
    mark(refs[-1])


def settle(*after):
    return pl.pallas_call(
        settle_kernel,
        in_specs=[STAY] * len(after),
        out_specs=pl.BlockSpec(memory_space=pltpu.VMEM),
        out_shape=TOKEN,
        compiler_params=pltpu.CompilerParams(vmem_limit_bytes=VMEM_LIMIT),
        cost_estimate=pl.CostEstimate(flops=1, bytes_accessed=44_000_000, transcendentals=0),
        name="settle",
    )(*after)


def assemble_kernel(groups, me_ref, tokens_ref, *refs):
    out_ref, token_ref = refs[-2:]
    width = out_ref.shape[2]
    mark(token_ref)
    for block in range(groups):
        out_ref[block] = tokens_ref[:, block * width : (block + 1) * width]
    out_ref[groups] = tokens_ref[:, pl.ds(pl.multiple_of(me_ref[0] * width, width), width)]
    for k in range(1, groups):
        out_ref[groups + k] = refs[k - 1][...]


def assemble(me, tokens, others, *after):
    groups = len(others) + 1
    rows, depth = tokens.shape
    width = depth // groups
    whole = pl.BlockSpec((rows, width), lambda i, me: (0, 0))
    return pl.pallas_call(
        functools.partial(assemble_kernel, groups),
        grid_spec=pltpu.PrefetchScalarGridSpec(
            num_scalar_prefetch=1,
            grid=(1,),
            in_specs=[pl.BlockSpec((rows, depth), lambda i, me: (0, 0))] + [whole] * (groups - 1)
            + [STAY] * len(after),
            out_specs=[
                pl.BlockSpec((2 * groups, rows, width), lambda i, me: (0, 0, 0)),
                TOKEN_SPEC,
            ],
        ),
        out_shape=[jax.ShapeDtypeStruct((2 * groups, rows, width), tokens.dtype), TOKEN],
        cost_estimate=BRIEF,
        compiler_params=pltpu.CompilerParams(vmem_limit_bytes=VMEM_LIMIT),
        name="assemble",
    )(me, tokens, *others, *after)


def partial_kernel(shares_ref, gate_ref, up_ref, *refs):
    *results, token_ref = refs[-1 - 2 * shares_ref.shape[1] :]
    ranks, groups, rows, width = shares_ref.shape
    shares = shares_ref[...].reshape(ranks * groups * rows, width)
    mark(token_ref)
    for which, weight_ref in enumerate((gate_ref, up_ref)):
        product = project(shares, weight_ref[...])
        product = product.reshape(ranks, groups, rows, product.shape[1])
        for k in range(groups):
            part = product[:, k].reshape(ranks * rows, product.shape[3])
            target_ref = results[which * groups + k]
            target_ref[...] = part.astype(target_ref.dtype)


def partial_products(gathered, outer_gate, outer_up, *after):
    ranks, doubled, rows, width = gathered.shape
    groups = doubled // 2
    unit_rows = outer_gate.shape[0]
    tile = tile_of(unit_rows)
    group_tok = ranks * rows
    weight = pl.BlockSpec((tile, width), lambda i: (i, 0))
    result = pl.BlockSpec((group_tok, tile), lambda i: (0, i))
    return pl.pallas_call(
        partial_kernel,
        grid=(unit_rows // tile,),
        in_specs=[
            pl.BlockSpec(
                (ranks, groups, rows, width),
                lambda i: (0, 1, 0, 0),
                pipeline_mode=pl.Buffered(1),
            ),
            weight,
            weight,
        ]
        + [STAY] * len(after),
        out_specs=[result] * (2 * groups) + [TOKEN_SPEC],
        out_shape=[
            jax.ShapeDtypeStruct(
                (group_tok, unit_rows), jnp.bfloat16 if k % 2 else jnp.float32
            )
            for _ in range(2)
            for k in range(groups)
        ]
        + [TOKEN],
        compiler_params=pltpu.CompilerParams(vmem_limit_bytes=VMEM_LIMIT),
        cost_estimate=BRIEF,
        name="partial_products",
    )(gathered, outer_gate, outer_up, *after)


def join_kernel(far_gate_ref, both_gate_ref, far_up_ref, both_up_ref, *refs):
    leave_gate_ref, leave_up_ref, token_ref = refs[-3:]
    mark(token_ref)
    for far_ref, both_ref, leave_ref in (
        (far_gate_ref, both_gate_ref, leave_gate_ref),
        (far_up_ref, both_up_ref, leave_up_ref),
    ):
        leave_ref[...] = (far_ref[...] + both_ref[...].astype(jnp.float32)).astype(
            leave_ref.dtype
        )


def join(parts, *after):
    group_tok, unit_rows = parts[0].shape
    tile = unit_rows // 2 if unit_rows % 256 == 0 else unit_rows
    block = pl.BlockSpec((group_tok, tile), lambda i: (0, i))
    leave = jax.ShapeDtypeStruct((group_tok, unit_rows), jnp.bfloat16)
    return pl.pallas_call(
        join_kernel,
        grid=(unit_rows // tile,),
        in_specs=[block] * len(parts) + [STAY] * len(after),
        out_specs=[block] * 2 + [TOKEN_SPEC],
        out_shape=[leave, leave, TOKEN],
        compiler_params=pltpu.CompilerParams(vmem_limit_bytes=VMEM_LIMIT),
        cost_estimate=BRIEF,
        name="join",
    )(*parts, *after)


def policy_kernel(blocks_ref, w_gate_ref, w_up_ref, *refs):
    gate_ref, up_ref, inputs_ref, token_ref, turned_ref = refs[-5:]
    ranks, groups, rows, width = blocks_ref.shape

    @pl.when(pl.program_id(0) == 0)
    def _():
        mark(token_ref)
        for block in range(groups):
            part = blocks_ref[:, block].reshape(ranks * rows, width)
            inputs_ref[:, block * width : (block + 1) * width] = part
            turned_ref[block * width : (block + 1) * width] = part.T

    turned = turned_ref[...]
    for weight_ref, result_ref in ((w_gate_ref, gate_ref), (w_up_ref, up_ref)):
        result_ref[...] = jnp.dot(
            weight_ref[0], turned, preferred_element_type=jnp.float32
        ).T


def policy_products(gathered, w_gate, w_up, *after):
    ranks, doubled, rows, width = gathered.shape
    groups = doubled // 2
    unit_rows, depth = w_gate.shape[1:]
    tile = tile_of(unit_rows)
    group_tok = ranks * rows
    weight = pl.BlockSpec((1, tile, depth), lambda i: (0, i, 0))
    result = pl.BlockSpec((group_tok, tile), lambda i: (0, i))
    return pl.pallas_call(
        policy_kernel,
        grid=(unit_rows // tile,),
        in_specs=[
            pl.BlockSpec(
                (ranks, groups, rows, width),
                lambda i: (0, 0, 0, 0),
                pipeline_mode=pl.Buffered(1),
            ),
            weight,
            weight,
        ]
        + [STAY] * len(after),
        out_specs=[result, result, pl.BlockSpec((group_tok, depth), lambda i: (0, 0)), TOKEN_SPEC],
        out_shape=[
            jax.ShapeDtypeStruct((group_tok, unit_rows), jnp.float32),
            jax.ShapeDtypeStruct((group_tok, unit_rows), jnp.float32),
            jax.ShapeDtypeStruct((group_tok, depth), gathered.dtype),
            TOKEN,
        ],
        scratch_shapes=[pltpu.VMEM((depth, group_tok), gathered.dtype)],
        compiler_params=pltpu.CompilerParams(vmem_limit_bytes=VMEM_LIMIT),
        cost_estimate=BRIEF,
        name="policy_products",
    )(gathered, w_gate, w_up, *after)


def grads_kernel(gate_ref, up_ref, readout_ref, token_grad_ref, inputs_ref, *refs):
    grad_gate_ref, grad_up_ref, token_ref = refs[-3:]
    mark(token_ref)
    gate = gate_ref[...]
    hidden_grad = token_grad_ref[...] * readout_ref[...].astype(jnp.float32)
    sigma = jax.nn.sigmoid(gate)
    gate_grad = hidden_grad * up_ref[...] * sigma * (1.0 + gate * (1.0 - sigma))
    up_grad = hidden_grad * (gate * sigma)
    contract = (((0,), (0,)), ((), ()))
    for target_ref, grad in ((grad_gate_ref, gate_grad), (grad_up_ref, up_grad)):
        target_ref[0] = lax.dot_general(
            grad.astype(jnp.bfloat16),
            inputs_ref[...],
            contract,
            preferred_element_type=jnp.float32,
        ).astype(target_ref.dtype)


def weight_grads(gate, upper, readout, token_grad, inputs, *after):
    group_tok, unit_rows = gate.shape
    depth = inputs.shape[1]
    tile = tile_of(unit_rows)
    units = pl.BlockSpec((group_tok, tile), lambda i: (0, i))
    result = pl.BlockSpec((1, tile, depth), lambda i: (0, i, 0))
    shape = jax.ShapeDtypeStruct((1, unit_rows, depth), jnp.bfloat16)
    return pl.pallas_call(
        grads_kernel,
        grid=(unit_rows // tile,),
        in_specs=[
            units,
            units,
            units,
            pl.BlockSpec((group_tok, 1), lambda i: (0, 0)),
            pl.BlockSpec(
                (group_tok, depth), lambda i: (0, 0), pipeline_mode=pl.Buffered(1)
            ),
        ]
        + [STAY] * len(after),
        out_specs=[result, result, TOKEN_SPEC],
        out_shape=[shape, shape, TOKEN],
        compiler_params=pltpu.CompilerParams(vmem_limit_bytes=VMEM_LIMIT),
        cost_estimate=BRIEF,
        name="weight_grads",
    )(gate, upper, readout, token_grad[:, None], inputs, *after)


def outer_kernel(groups, strip, me_ref, outer_ref, moment_ref, *refs):
    del me_ref
    inner = (refs[0].at[0], *refs[1:groups])
    new_outer_ref, new_moment_ref, token_ref = refs[-3:]
    rows, width = outer_ref.shape
    mark(token_ref)

    def step(index, carry):
        at = pl.ds(pl.multiple_of(index * strip, strip), strip)
        for block in range(width // BLOCK):
            cols = pl.ds(block * BLOCK, BLOCK)
            outer = outer_ref[at, cols].astype(jnp.float32)
            total = jnp.zeros_like(outer)
            for ref in inner:
                delta = outer - ref[at, cols].astype(jnp.float32)
                top = jnp.max(jnp.abs(delta), axis=1, keepdims=True)
                scale = (top + tiny_eps).astype(jnp.bfloat16).astype(jnp.float32)
                levels = (delta * (1.0 / scale)).astype(jnp.bfloat16)
                total = total + levels.astype(jnp.float32) * scale
            average = total * (1.0 / groups)
            new_moment = outer_mu * moment_ref[at, cols] + average
            new_moment_ref[at, cols] = new_moment
            new_outer_ref[at, cols] = (
                outer - outer_rate * (average + outer_mu * new_moment)
            ).astype(new_outer_ref.dtype)
        return carry

    lax.fori_loop(0, rows // strip, step, 0)


def outer_update(first, steps, tile, me, outer, moment, weight, pieces, previous, *after):
    width = outer.shape[1]
    strip = 32 if tile % 32 == 0 else 16
    groups = len(pieces) + 1
    placed = pl.BlockSpec((tile, width), lambda i, me: (first + i, 0))
    in_specs = [
        placed,
        placed,
        pl.BlockSpec((1, tile, width), lambda i, me: (0, first + i, me[0])),
    ] + [
        pl.BlockSpec((tile, width), lambda i, me, skip=first - begin: (skip + i, 0))
        for _, begin in pieces
    ]
    args = [me, outer, moment, weight] + [piece for piece, _ in pieces]
    aliases = {}
    if previous is not None:
        aliases = {len(args): 0, len(args) + 1: 1}
        in_specs += [STAY] * 2
        args += list(previous)
    in_specs += [STAY] * len(after)
    args += list(after)
    *updated, token = pl.pallas_call(
        functools.partial(outer_kernel, groups, strip),
        grid_spec=pltpu.PrefetchScalarGridSpec(
            num_scalar_prefetch=1,
            grid=(steps,),
            in_specs=in_specs,
            out_specs=[placed, placed, TOKEN_SPEC],
        ),
        out_shape=[
            jax.ShapeDtypeStruct(outer.shape, outer.dtype),
            jax.ShapeDtypeStruct(moment.shape, moment.dtype),
            TOKEN,
        ],
        input_output_aliases=aliases,
        cost_estimate=BRIEF,
        compiler_params=pltpu.CompilerParams(vmem_limit_bytes=VMEM_LIMIT),
        name="outer_update",
    )(*args)
    return updated, token


def per_device(tokens, readout, resp_mask, order, w_gate, w_up, outer_gate, outer_up, moment):
    groups = lax.axis_size("rep")
    ranks = lax.axis_size("fsdp")
    place = lax.axis_index("rep").reshape(1).astype(jnp.int32)
    width = outer_gate.shape[1]

    def swap(value, bits):
        return lax.ppermute(value, "rep", [(i, i ^ bits) for i in range(groups)])

    tile = outer_gate.shape[0] // TILES
    pieces = []
    updated = None

    def send(begin, steps, masks, *after):
        parts, token = pick(begin, steps, tile, place, w_gate, masks, width, *after)
        came = [swap(part, mask) for part, mask in zip(parts, masks)]
        pieces.extend((mask, begin, steps, piece) for mask, piece in zip(masks, came))
        return came, token

    def update(first, steps, *after):
        there = [
            (piece, begin)
            for mask, begin, count, piece in pieces
            if begin <= first and first + steps <= begin + count
        ]
        assert len(there) == groups - 1
        return outer_update(
            first, steps, tile, place, outer_gate, moment, w_gate, there, updated, *after
        )

    early, token = send(0, 10, (2,))
    shares, token = pick(
        0, 1, tokens.shape[0], place, tokens[None], tuple(range(1, groups)), width, token
    )
    others = [swap(share, bits) for bits, share in enumerate(shares, 1)]
    assembled, token = assemble(place, tokens, others, token)
    gathered = lax.all_gather(assembled, "fsdp", axis=0, tiled=False)
    (near, _), token = send(0, 6, (1, 3), token)

    *parts, token = partial_products(gathered, outer_gate, outer_up, settle(token, near, *early))
    for at in (1, 3, 5, 7):
        parts[at] = swap(parts[at], 1)
    stay_gate, near_gate, far_gate, both_gate, stay_up, near_up, far_up, both_up = parts
    leave_gate, leave_up, token = join(
        (far_gate, both_gate, far_up, both_up), near_gate, near_up
    )
    gate_ref, upper_ref = (
        stay + near.astype(jnp.float32) + swap(leave, 2).astype(jnp.float32)
        for stay, near, leave in (
            (stay_gate, near_gate, leave_gate),
            (stay_up, near_up, leave_up),
        )
    )
    _, token = send(6, 4, (1, 3), token)
    gate, upper, inputs, token = policy_products(gathered, w_gate, w_up, token)
    updated, token = update(0, 6, token)

    group_tok = inputs.shape[0]
    seqs = group_tok // LEN
    mask_f = resp_mask.astype(jnp.float32)
    hidden = (jax.nn.silu(gate) * upper).astype(jnp.bfloat16)
    hidden_ref = (jax.nn.silu(gate_ref) * upper_ref).astype(jnp.bfloat16)
    relative = local_scores(hidden, readout, mask_f, seqs) - local_scores(
        hidden_ref, readout, mask_f, seqs
    )
    _, token = send(10, 2, (1, 2, 3), token, relative[None])
    hop = 1
    while hop < ranks:
        relative = relative + lax.ppermute(
            relative, "fsdp", [(i, i ^ hop) for i in range(ranks)]
        )
        hop *= 2
    places = jnp.arange(seqs, dtype=jnp.int32)
    pick_chosen = (order[0, 0::2][:, None] == places[None, :]).astype(jnp.float32)
    pick_rejected = (order[0, 1::2][:, None] == places[None, :]).astype(jnp.float32)
    highest = lax.Precision.HIGHEST
    margin = dpo_beta * (
        jnp.dot(pick_chosen, relative, precision=highest)
        - jnp.dot(pick_rejected, relative, precision=highest)
    )
    loss = jnp.mean(jax.nn.softplus(-margin)).reshape(1)
    weight = dpo_beta * jax.nn.sigmoid(-margin) / pick_chosen.shape[0]
    coef = jnp.dot(weight, pick_rejected - pick_chosen, precision=highest)
    token_grad = jnp.broadcast_to(coef[:, None], (seqs, LEN)).reshape(-1) * mask_f
    grad_gate, grad_up, token = weight_grads(gate, upper, readout, token_grad, inputs, token)
    _, token = send(12, 1, (1, 2, 3), token)
    updated, token = update(6, 4, token)
    _, token = send(13, 1, (1, 2, 3), token)
    updated, token = update(10, 2, token)
    updated, token = update(12, 1, token)
    updated, token = update(13, 1, token)
    new_outer, new_moment = updated
    return (loss, grad_gate, grad_up, new_outer, new_moment)


def solution(mesh):
    return jax.shard_map(
        per_device,
        mesh=mesh,
        in_specs=(
            P(("rep", "fsdp"), None),
            P("rep", "fsdp"),
            P("rep"),
            P("rep", None),
            P("rep", "fsdp", None),
            P("rep", "fsdp", None),
            P("fsdp", "rep"),
            P("fsdp", "rep"),
            P("fsdp", "rep"),
        ),
        out_specs=(
            P("rep"),
            P("rep", "fsdp", None),
            P("rep", "fsdp", None),
            P("fsdp", "rep"),
            P("fsdp", "rep"),
        ),
        check_vma=False,
    )
```
